32 devices in a mesh: lat: 4 (over x, core), dp: 8 (over z, y).
Axes of the slice: x: 2, y: 2, z: 4, core: 2. Of those that a mesh axis runs over, the one named last changes fastest.
Arguments:
- inputs: bfloat16 [8, 4, 128, 384], P('dp', 'lat'), may hold values from -6 to 6
- cotangent: bfloat16 [8, 4, 128, 384], P('dp', 'lat'), may hold values from -6 to 6
- kernel_tiles: bfloat16 [4, 6, 3, 128, 128], P('lat'), may hold values from -0.21875 to 0.21875
- mix_weight: bfloat16 [1152, 384], replicated, may hold values from -0.1875 to 0.1875
- slot_row: int32 [4, 6], P('lat'), may hold values from -1 to 1, as said below
- slot_lon: int32 [4, 6], P('lat'), may hold values from -1 to 1
- slot_count: int32 [4], P('lat'), may hold values from 3 to 6, as said below
- scale_exps: int32 [1152, 3], P('dp'), may hold values from -1 to 1
Outputs:
- block_out: bfloat16 [8, 4, 128, 384], P('dp', 'lat')
- input_grad: bfloat16 [8, 4, 128, 384], P('dp', 'lat')
- weight_grad: float32 [1152, 384], P('dp')
The draws below stay inside these ranges and needn't reach their ends.
Inputs may be any that keep to these rules, and one draw needn't show every extreme that they name: `slot_row`: slot 0 of every row has offset 0, slot 1 offset -1 and slot 2 offset +1. `slot_count`: 6 at the first and the last row; fewer at the other rows.
All inputs are finite; a program needn't handle non-finite values.
Results may differ from the reference program's by a relative error of at most 0.0095.
Values may be sent and summed in bfloat16 or wider, within the bound.
A program may use at most 64 MiB of HBM per device.

```python
import math
import jax
import jax.numpy as jnp
from jax import lax

C = 384
K = 3
BLK = 128
SLOTS = 6
NBLK = 1
LON = 128
LAT = 4
SAMPLES = 8


def draw_slot_row(key, part):
    key = jax.random.fold_in(key, 11)
    others = jax.random.randint(key, (LAT, SLOTS - 3), -1, 2).astype(jnp.int32)
    leading = jnp.broadcast_to(jnp.array([0, -1, 1], dtype=jnp.int32), (LAT, 3))
    return jnp.concatenate([leading, others], axis=1)


def draw_slot_lon(key, part):
    key = jax.random.fold_in(key, 12)
    return jax.random.randint(key, (LAT, SLOTS), -1, 2).astype(jnp.int32)


def draw_slot_count(key, part):
    key = jax.random.fold_in(key, 13)
    row_ids = jnp.arange(LAT, dtype=jnp.int32)
    nearest = jnp.minimum(row_ids, LAT - 1 - row_ids)
    base_count = SLOTS - (SLOTS - 3) * 2 * nearest // LAT
    jitter = jax.random.randint(key, (LAT,), -1, 2).astype(jnp.int32)
    counted = jnp.clip(base_count + jitter, 3, SLOTS - 1)
    return jnp.where(nearest == 0, SLOTS, counted).astype(jnp.int32)


def touch_ends(values, key, least, largest):
    extent = values.shape
    index_at = [jax.random.randint(jax.random.fold_in(key, axis), (), 0, extent[axis]) for axis in range(len(extent))]
    values = values.at[tuple(index_at)].set(least)
    longest = extent.index(max(extent))
    index_at[longest] = (index_at[longest] + 1) % extent[longest]
    return values.at[tuple(index_at)].set(largest)


def strengthened(values, rng, source, target, shards_of, factor):
    def block_of(axis_at):
        return (jnp.arange(values.shape[axis_at]) // (values.shape[axis_at] // shards_of)).reshape((-1,) + (1,) * (values.ndim - 1 - axis_at))

    near = jax.random.permutation(rng, shards_of)[block_of(target)]
    second = (block_of(target) + shards_of // 2) % shards_of
    return jnp.where((block_of(source) == near) | (block_of(source) == second), factor * values, values)


def level_of(rng, extent, split, low, top_value):
    loudness, own = 1.0, jax.random.fold_in(rng, 6)
    for axis_at, shards_of in split:
        draws = jnp.exp(jax.random.uniform(jax.random.fold_in(own, axis_at), (shards_of,), jnp.float32, low / len(split), top_value / len(split)))
        loudness = loudness * jnp.repeat(draws, extent[axis_at] // shards_of).reshape([-1 if axis == axis_at else 1 for axis in range(len(extent))])
    return loudness


def gaussian(rng, dims, spread, reach, cuts=(), kind=jnp.bfloat16):
    drawn = jax.random.normal(rng, dims, jnp.float32) * spread
    if len(cuts) > 0:
        drawn = level_of(rng, dims, cuts, -0.22, 0.18) * drawn
    return jnp.clip(drawn, min=-reach, max=reach).astype(kind)


def bell_draw_with(key, dims, width, limit, cuts, heavy, kind=jnp.bfloat16):
    values = width * jax.random.normal(key, dims, jnp.float32)
    if cuts:
        values = values * level_of(key, dims, cuts, -0.22, 0.18)
    return jnp.clip(strengthened(values, jax.random.fold_in(key, 3), *heavy), -limit, limit).astype(kind)


def setup_inputs(seed: int = 0) -> dict:
    streams_of = jax.random.split(jax.random.key(seed), 9)
    inputs = bell_draw_with(streams_of[0], (SAMPLES, LAT, LON, C), 1.0, 6.0, ((0, 8), (1, 4)), (0, 3, 8, 2.0))
    cotangent = gaussian(streams_of[1], (SAMPLES, LAT, LON, C), 1.0, 6.0, ((0, 8), (1, 4)))
    kernel_tiles = gaussian(streams_of[2], (LAT, SLOTS, K, BLK, BLK), (BLK * SLOTS) ** -0.5, 0.21875, ((0, 4),))
    mix_weight = gaussian(streams_of[3], (C * K, C), (C * K) ** -0.5, 0.1875)
    slot_row = draw_slot_row(jax.random.fold_in(streams_of[8], 71), 0)
    slot_lon = draw_slot_lon(jax.random.fold_in(streams_of[8], 71), 0)
    slot_count = draw_slot_count(jax.random.fold_in(streams_of[8], 71), 0)
    scale_exps = touch_ends(jax.random.randint(streams_of[7], (C * K, C // BLK), -1, 2), jax.random.fold_in(streams_of[7], 1), -1, 1).astype(jnp.int32)
    return dict(inputs=inputs, cotangent=cotangent, kernel_tiles=kernel_tiles, mix_weight=mix_weight, slot_row=slot_row, slot_lon=slot_lon, slot_count=slot_count, scale_exps=scale_exps)


def disco(field, kernel_tiles, slot_row, slot_lon, slot_count):
    blocks = field.reshape(LAT, NBLK, BLK, C)
    padded = jnp.pad(blocks, ((1, 1), (0, 0), (0, 0), (0, 0)))
    row_ids = jnp.arange(LAT, dtype=jnp.int32)
    blk_ids = jnp.arange(NBLK, dtype=jnp.int32)
    accum = jnp.zeros((LAT, NBLK, BLK, C, K), jnp.float32)
    for slot_index in range(SLOTS):
        source = (row_ids + slot_row[:, slot_index] + 1).astype(jnp.int32)
        shifted = ((blk_ids[None, :] + slot_lon[:, slot_index][:, None]) % NBLK).astype(jnp.int32)
        picked = padded[source[:, None], shifted]
        keep_mask = (slot_index < slot_count).astype(jnp.float32)
        tiles = kernel_tiles[:, slot_index].astype(jnp.float32) * keep_mask[:, None, None, None]
        accum = accum + jnp.einsum('rkpq,rjqc->rjpck', tiles, picked.astype(jnp.float32))
    return accum.reshape(LAT * LON, C * K)

def reference(inputs, cotangent, kernel_tiles, mix_weight, slot_row, slot_lon, slot_count, scale_exps):

    def one_sample(pair):
        field, cot = pair
        field_f = field.astype(jnp.float32)
        basis_mat, pullback = jax.vjp(lambda f: disco(f, kernel_tiles, slot_row, slot_lon, slot_count), field_f)
        basis_out = basis_mat.astype(jnp.bfloat16)
        mixed = jnp.dot(basis_out, mix_weight, preferred_element_type=jnp.float32)
        gate_value = jax.nn.sigmoid(mixed)
        flat_in = field_f.reshape(LAT * LON, C)
        result = (flat_in + mixed * gate_value).astype(jnp.bfloat16)
        flat_cot = cot.reshape(LAT * LON, C).astype(jnp.float32)
        dmixed = (flat_cot * gate_value * (1.0 + mixed * (1.0 - gate_value))).astype(jnp.bfloat16)
        dbasis = lax.dot_general(dmixed, mix_weight, (((1,), (1,)), ((), ())), preferred_element_type=jnp.float32).astype(jnp.bfloat16)
        back = pullback(dbasis.astype(jnp.float32))[0]
        grad_in = (cot.astype(jnp.float32) + back).astype(jnp.bfloat16)
        partial_value = lax.dot_general(basis_out, dmixed, (((0,), (0,)), ((), ())), preferred_element_type=jnp.float32)
        return (result.reshape(LAT, LON, C), grad_in, partial_value)
    block_out, input_grad, partials = lax.map(one_sample, (inputs, cotangent))
    grad_total = lax.optimization_barrier(jnp.sum(partials, axis=0))
    factor = jnp.repeat(jnp.exp2(-scale_exps.astype(jnp.float32)), BLK, axis=1)
    weight_grad = grad_total * factor / math.sqrt(SAMPLES * LAT * LON)
    return (block_out, input_grad, weight_grad)
```

```python
import math

import jax
import jax.numpy as jnp
from jax import lax
from jax.experimental import pallas as pl
from jax.experimental.pallas import tpu as pltpu
from jax.sharding import PartitionSpec as P


def extended_2(cells, sides, width):
    for axis, dim in sides:
        count = lax.axis_size(axis)
        ends = count - 1
        head = lax.slice_in_dim(cells, 0, width, axis=dim)
        tail = lax.slice_in_dim(cells, cells.shape[dim] - width, cells.shape[dim], axis=dim)
        cells = jnp.concatenate(
            [
                lax.ppermute(tail, axis, [(i, (i + 1) % count) for i in range(ends)]),
                cells,
                lax.ppermute(head, axis, [((i + 1) % count, i) for i in range(ends)]),
            ],
            axis=dim,
        )
    return cells


def local(inputs, cotangent, kernel_tiles, mix_weight, slot_row, slot_lon, slot_count, scale_exps):
    rows_here = inputs.shape[1]
    lon_width = inputs.shape[2]
    channels = inputs.shape[3]
    slot_total = kernel_tiles.shape[1]
    basis_count = kernel_tiles.shape[2]
    tile_size = kernel_tiles.shape[3]
    lon_blocks = lon_width // tile_size
    points = rows_here * lon_width
    mix_major = (
        mix_weight.reshape(channels, basis_count, channels)
        .transpose(1, 0, 2)
        .reshape(basis_count * channels, channels)
    )
    extended = extended_2(inputs, (("lat", 1),), 1)
    blocks = extended[0].reshape(rows_here + 2, lon_blocks, tile_size, channels)
    row_ids = jnp.arange(rows_here, dtype=jnp.int32)
    blk_ids = jnp.arange(lon_blocks, dtype=jnp.int32)
    sources = []
    shifts = []
    masked = []
    for slot_index in range(slot_total):
        sources.append(row_ids + slot_row[:, slot_index] + 1)
        shifts.append((blk_ids[None, :] + slot_lon[:, slot_index][:, None]) % lon_blocks)
        keep_mask = (slot_index < slot_count).astype(jnp.bfloat16)
        masked.append(kernel_tiles[:, slot_index] * keep_mask[:, None, None, None])
    accum = jnp.zeros((rows_here, lon_blocks, tile_size, basis_count, channels), jnp.float32)
    for slot_index in range(slot_total):
        picked = blocks[sources[slot_index][:, None], shifts[slot_index]]
        accum = accum + jnp.einsum(
            "rkpq,rjqc->rjpkc", masked[slot_index], picked, preferred_element_type=jnp.float32
        )
    basis_out = accum.reshape(points, basis_count * channels).astype(jnp.bfloat16)
    mixed = jnp.dot(basis_out, mix_major, preferred_element_type=jnp.float32)
    gate_value = jax.nn.sigmoid(mixed)
    flat_in = inputs.reshape(points, channels).astype(jnp.float32)
    result = (flat_in + mixed * gate_value).astype(jnp.bfloat16).reshape(inputs.shape)
    flat_cot = cotangent.reshape(points, channels).astype(jnp.float32)
    dmixed = (flat_cot * gate_value * (1.0 + mixed * (1.0 - gate_value))).astype(jnp.bfloat16)
    dbasis = lax.dot_general(
        dmixed, mix_major, (((1,), (1,)), ((), ())), preferred_element_type=jnp.float32
    ).astype(jnp.bfloat16)
    dbasis = dbasis.reshape(rows_here, lon_blocks, tile_size, basis_count, channels)
    back_ext = jnp.zeros((rows_here + 2, lon_blocks, tile_size, channels), jnp.float32)
    for slot_index in range(slot_total):
        slot_term = jnp.einsum(
            "rkpq,rjpkc->rjqc", masked[slot_index], dbasis, preferred_element_type=jnp.float32
        )
        back_ext = back_ext.at[sources[slot_index][:, None], shifts[slot_index]].add(slot_term)
    rim_rows = jnp.concatenate([back_ext[:1], back_ext[rows_here + 1 :]], axis=0).reshape(
        2, lon_width, channels
    )
    returned = extended_2(rim_rows.astype(jnp.bfloat16), (("lat", 0),), 1).astype(rim_rows.dtype)
    inner_grad = back_ext[1 : rows_here + 1].reshape(rows_here, lon_width, channels)
    inner_grad = inner_grad.at[0].add(returned[0])
    inner_grad = inner_grad.at[rows_here - 1].add(returned[3])
    grad_in = (cotangent[0].astype(jnp.float32) + inner_grad).astype(jnp.bfloat16)[None]
    major_part = lax.dot_general(
        basis_out, dmixed, (((0,), (0,)), ((), ())), preferred_element_type=jnp.float32
    )
    partial_value = (
        major_part.reshape(basis_count, channels, channels)
        .transpose(1, 0, 2)
        .reshape(channels * basis_count, channels)
    )
    row_part = lax.psum_scatter(partial_value, "dp", scatter_dimension=0, tiled=True)
    grad_total = lax.psum(row_part, "lat")
    factor = jnp.repeat(jnp.exp2(-scale_exps.astype(jnp.float32)), tile_size, axis=1)
    count_all = lax.axis_size("dp") * inputs.shape[0] * lax.axis_size("lat") * rows_here * lon_width
    weight_grad = grad_total * factor / math.sqrt(count_all)
    return (result, grad_in, weight_grad)


MESH = pl.DeviceIdType.MESH
TILE = 16
LANES = 128


def dot(a, b, da, db):
    return lax.dot_general(a, b, (((da,), (db,)), ((), ())), preferred_element_type=jnp.float32)


def fused(
    row_ref, count_ref, scale_ref, x_hbm, cot_hbm, tiles_hbm, w_hbm,
    out_ref, gin_ref, wg_ref,
    xs, cot, tiles, w, wk, tmat, bas, dmix, dbas, back, rim, gt, r1, s1, r2, q, gk,
    load_sem, halo_s, halo_r, fac_s, fac_r, xy_s, xy_r, rim_s, rim_r, z_s, z_r, lat_s, lat_r,
):
    lat = lax.axis_index("lat")
    dp = lax.axis_index("dp")
    last = 3
    x, c = lat // 2, lat % 2
    z, y = dp // 2, dp % 2
    slots, basis = tiles.shape[0], tiles.shape[1]
    size = tiles.shape[2]
    chans = w.shape[1]
    f32, bf16 = jnp.float32, jnp.bfloat16

    loads = [
        pltpu.make_async_copy(tiles_hbm.at[0], tiles, load_sem.at[0]),
        pltpu.make_async_copy(w_hbm, w, load_sem.at[1]),
        pltpu.make_async_copy(x_hbm.at[0, 0], xs.at[0], load_sem.at[2]),
        pltpu.make_async_copy(cot_hbm.at[0, 0], cot, load_sem.at[3]),
    ]
    barrier = pltpu.get_barrier_semaphore()
    x_lat = (1 - x) * 2 + c
    c_lat = x * 2 + (1 - c)
    xc_lat = 3 - lat
    y_dp = z * 2 + (1 - y)
    z_dps = [((z + o) % 4) * 2 + y for o in (1, 2, 3)]
    friends = [(x_lat, dp), (c_lat, dp), (xc_lat, dp), (lat, y_dp), (x_lat, y_dp)]
    friends += [(lat, d) for d in z_dps]
    for friend in friends:
        pl.semaphore_signal(barrier, inc=1, device_id=friend, device_id_type=MESH)
    loads[2].start()
    loads[0].start()
    loads[1].start()
    loads[3].start()
    pl.semaphore_wait(barrier, len(friends))

    def remote(src, dst, send, recv, target):
        return pltpu.make_async_remote_copy(
            src_ref=src, dst_ref=dst, send_sem=send, recv_sem=recv,
            device_id=target, device_id_type=MESH,
        )

    down = remote(x_hbm.at[0, 0], xs.at[1], halo_s.at[0], halo_r.at[0], (lat + 1, dp))
    up = remote(x_hbm.at[0, 0], xs.at[2], halo_s.at[1], halo_r.at[1], (lat - 1, dp))

    @pl.when(lat < last)
    def _():
        down.start()

    @pl.when(lat > 0)
    def _():
        up.start()

    @pl.when(lat == 0)
    def _():
        xs[1] = jnp.zeros(xs.shape[1:], bf16)
        rim[2] = jnp.zeros(rim.shape[1:], bf16)

    @pl.when(lat == last)
    def _():
        xs[2] = jnp.zeros(xs.shape[1:], bf16)
        rim[3] = jnp.zeros(rim.shape[1:], bf16)

    gt[:, 3, :, 96:112, :] = jnp.zeros((2, 4, TILE, LANES), bf16)

    loads[0].wait()
    count = count_ref[0]
    offs = (0, -1, 1)
    weight = [
        [jnp.where(jnp.logical_and(row_ref[0, s] == d, s < count), 1.0, 0.0).astype(f32) for s in range(3, slots)]
        for d in offs
    ]
    for k in range(basis):
        extra = [tiles[s, k].astype(f32) for s in range(3, slots)]
        for n in range(3):
            total = tiles[n, k].astype(f32)
            for t, e in zip(weight[n], extra):
                total = total + t * e
            tmat[k * size : (k + 1) * size, n * size : (n + 1) * size] = total.astype(bf16)

    loads[1].wait()
    blk = 64
    r = lax.broadcasted_iota(jnp.int32, (basis * blk, basis * blk), 0)
    col = lax.broadcasted_iota(jnp.int32, (basis * blk, basis * blk), 1)
    kk = (r >= blk).astype(jnp.int32) + (r >= 2 * blk).astype(jnp.int32)
    perm = jnp.where(col == 3 * (r - blk * kk) + kk, 1.0, 0.0).astype(bf16)
    for b in range(chans // blk):
        part = dot(perm, w[b * basis * blk : (b + 1) * basis * blk, :], 1, 0).astype(bf16)
        for k in range(basis):
            wk[k, b * blk : (b + 1) * blk, :] = part[k * blk : (k + 1) * blk, :]

    loads[2].wait()
    loads[3].wait()

    @pl.when(lat > 0)
    def _():
        down.wait_recv()

    @pl.when(lat < last)
    def _():
        up.wait_recv()

    bas[0] = dot(tmat[...], xs[...].reshape(3 * size, chans), 1, 0).astype(bf16)
    send_bas = remote(bas.at[0], bas.at[1], fac_s.at[0], fac_r.at[0], (c_lat, dp))
    send_bas.start()
    mixed = dot(bas[0, 0:size, :], wk[0], 1, 0)
    for k in range(1, basis):
        mixed = mixed + dot(bas[0, k * size : (k + 1) * size, :], wk[k], 1, 0)
    gate = jax.nn.sigmoid(mixed)
    dmix[0] = (cot[...].astype(f32) * gate * (1.0 + mixed * (1.0 - gate))).astype(bf16)
    send_dmix = remote(dmix.at[0], dmix.at[1], fac_s.at[1], fac_r.at[1], (c_lat, dp))
    send_dmix.start()
    out_ref[0, 0] = (xs[0].astype(f32) + mixed * gate).astype(bf16)

    dm = dmix[0]
    for k in range(basis):
        dbas[k * size : (k + 1) * size, :] = dot(dm, wk[k], 1, 1).astype(bf16)

    send_bas.wait_recv()
    send_dmix.wait_recv()
    both = dmix[...].reshape(2 * size, chans)
    for k in range(basis):
        lhs = jnp.concatenate([bas[0, k * size : (k + 1) * size, :], bas[1, k * size : (k + 1) * size, :]], axis=0)
        grad = dot(lhs, both, 0, 0).astype(bf16)
        for d in range(8):
            for i in range(3):
                for j in range(3):
                    part, at = divmod((k * 3 + i) * 3 + j, 7)
                    lo = 48 * d + TILE * i
                    gt[d % 2, part, d // 2, at * TILE : (at + 1) * TILE, :] = grad[
                        lo : lo + TILE, j * LANES : (j + 1) * LANES
                    ]

    xy = [
        remote(gt.at[1 - y, x_lat], r1.at[2], xy_s.at[2], xy_r.at[2], (x_lat, y_dp)),
        remote(gt.at[y, x_lat], r1.at[0], xy_s.at[0], xy_r.at[0], (x_lat, dp)),
        remote(gt.at[1 - y, lat], r1.at[1], xy_s.at[1], xy_r.at[1], (lat, y_dp)),
    ]
    for copy in xy:
        copy.start()

    back[...] = dot(tmat[...], dbas[...], 0, 0)
    rim[0] = back[size : 2 * size, :].astype(bf16)
    rim[1] = back[2 * size : 3 * size, :].astype(bf16)
    rim_up = remote(rim.at[0], rim.at[3], rim_s.at[0], rim_r.at[0], (lat - 1, dp))
    rim_down = remote(rim.at[1], rim.at[2], rim_s.at[1], rim_r.at[1], (lat + 1, dp))

    @pl.when(lat > 0)
    def _():
        rim_up.start()

    @pl.when(lat < last)
    def _():
        rim_down.start()

    for copy in xy:
        copy.wait_recv()
    own = gt.at[y, lat]
    for n in range(4):
        s1[n] = (
            own[n].astype(f32) + r1[0, n].astype(f32) + (r1[1, n].astype(f32) + r1[2, n].astype(f32))
        ).astype(bf16)
    zs = [
        remote(s1.at[(z + o) % 4], r2.at[o - 1], z_s.at[o - 1], z_r.at[o - 1], (lat, z_dps[o - 1]))
        for o in (1, 2, 3)
    ]
    for copy in zs:
        copy.start()

    @pl.when(lat < last)
    def _():
        rim_up.wait_recv()

    @pl.when(lat > 0)
    def _():
        rim_down.wait_recv()

    gin_ref[0, 0] = (
        cot[...].astype(f32) + back[0:size, :] + rim[2].astype(f32) + rim[3].astype(f32)
    ).astype(bf16)

    for copy in zs:
        copy.wait_recv()
    q[lat] = (
        s1[z].astype(f32) + r2[0].astype(f32) + (r2[1].astype(f32) + r2[2].astype(f32))
    ).astype(bf16)
    lats = [
        remote(q.at[lat], q.at[lat], lat_s.at[n], lat_r.at[n], (other, dp))
        for n, other in enumerate((x_lat, c_lat, xc_lat))
    ]
    arrive = [
        remote(q.at[other], q.at[other], lat_s.at[n], lat_r.at[n], (other, dp))
        for n, other in enumerate((x_lat, c_lat, xc_lat))
    ]
    for n in (2, 0, 1):
        lats[n].start()
    rr = lax.broadcasted_iota(jnp.int32, (144, 144), 0)
    cc = lax.broadcasted_iota(jnp.int32, (144, 144), 1)
    kc = (cc >= 48).astype(jnp.int32) + (cc >= 96).astype(jnp.int32)
    order = jnp.where(rr == 3 * (cc - 48 * kc) + kc, 1.0, 0.0).astype(bf16)
    factor = jnp.exp2(-scale_ref[...].astype(f32)) * (1.0 / math.sqrt(4 * 8 * size))
    for copy in arrive:
        copy.wait_recv()
    for t in range(27):
        part, at = divmod(t, 7)
        g, j = divmod(t, 3)
        gk[g * TILE : (g + 1) * TILE, j * LANES : (j + 1) * LANES] = q[part, at * TILE : (at + 1) * TILE, :]
    grad = dot(order, gk[...], 1, 0)
    for j in range(3):
        wg_ref[:, j * LANES : (j + 1) * LANES] = grad[:, j * LANES : (j + 1) * LANES] * factor[:, j : j + 1]

    @pl.when(lat < last)
    def _():
        down.wait_send()
        rim_down.wait_send()

    @pl.when(lat > 0)
    def _():
        up.wait_send()
        rim_up.wait_send()

    for copy in [send_bas, send_dmix] + xy + zs + lats:
        copy.wait_send()


def local_fused(inputs, cotangent, kernel_tiles, mix_weight, slot_row, slot_lon, slot_count, scale_exps):
    size, chans = inputs.shape[2], inputs.shape[3]
    basis = kernel_tiles.shape[2]
    bf16, f32 = jnp.bfloat16, jnp.float32
    dma = pltpu.SemaphoreType.DMA
    vmem = pl.BlockSpec(memory_space=pltpu.VMEM)
    smem = pl.BlockSpec(memory_space=pltpu.SMEM)
    hbm = pl.BlockSpec(memory_space=pl.ANY)
    return pl.pallas_call(
        fused,
        out_shape=(
            jax.ShapeDtypeStruct(inputs.shape, bf16),
            jax.ShapeDtypeStruct(inputs.shape, bf16),
            jax.ShapeDtypeStruct((basis * chans // 8, chans), f32),
        ),
        in_specs=[smem, smem, vmem, hbm, hbm, hbm, hbm],
        out_specs=(vmem, vmem, vmem),
        scratch_shapes=[
            pltpu.VMEM((3, size, chans), bf16),
            pltpu.VMEM((size, chans), bf16),
            pltpu.VMEM(kernel_tiles.shape[1:], bf16),
            pltpu.VMEM(mix_weight.shape, bf16),
            pltpu.VMEM((basis, chans, chans), bf16),
            pltpu.VMEM((basis * size, 3 * size), bf16),
            pltpu.VMEM((2, basis * size, chans), bf16),
            pltpu.VMEM((2, size, chans), bf16),
            pltpu.VMEM((basis * size, chans), bf16),
            pltpu.VMEM((3 * size, chans), f32),
            pltpu.VMEM((4, size, chans), bf16),
            pltpu.VMEM((2, 4, 4, 7 * TILE, LANES), bf16),
            pltpu.VMEM((3, 4, 7 * TILE, LANES), bf16),
            pltpu.VMEM((4, 7 * TILE, LANES), bf16),
            pltpu.VMEM((3, 7 * TILE, LANES), bf16),
            pltpu.VMEM((4, 7 * TILE, LANES), bf16),
            pltpu.VMEM((144, chans), bf16),
            dma((4,)), dma((2,)), dma((2,)), dma((2,)), dma((2,)), dma((3,)), dma((3,)),
            dma((2,)), dma((2,)), dma((3,)), dma((3,)), dma((3,)), dma((3,)),
        ],
        compiler_params=pltpu.CompilerParams(
            collective_id=0, has_side_effects=True, vmem_limit_bytes=40 * 1024 * 1024
        ),
        cost_estimate=pl.CostEstimate(flops=10**9, bytes_accessed=3 * 10**6, transcendentals=50000),
    )(slot_row, slot_count, scale_exps, inputs, cotangent, kernel_tiles, mix_weight)


def fits(mesh):
    return mesh.shape["lat"] == 4 and mesh.shape["dp"] == 8


def solution(mesh):
    in_specs = (
        P("dp", "lat", None, None),
        P("dp", "lat", None, None),
        P("lat", None, None, None, None),
        P(),
        P("lat", None),
        P("lat", None),
        P("lat"),
        P("dp", None),
    )
    out_specs = (P("dp", "lat", None, None), P("dp", "lat", None, None), P("dp", None))
    body = local_fused if fits(mesh) else local
    return jax.shard_map(body, mesh=mesh, in_specs=in_specs, out_specs=out_specs, check_vma=False)
```

```python
import math

import jax
import jax.numpy as jnp
from jax import lax
from jax.experimental import pallas as pl
from jax.experimental.pallas import tpu as pltpu
from jax.sharding import PartitionSpec as P


def extended_2(cells, sides, width):
    for axis, dim in sides:
        count = lax.axis_size(axis)
        ends = count - 1
        head = lax.slice_in_dim(cells, 0, width, axis=dim)
        tail = lax.slice_in_dim(cells, cells.shape[dim] - width, cells.shape[dim], axis=dim)
        cells = jnp.concatenate(
            [
                lax.ppermute(tail, axis, [(i, (i + 1) % count) for i in range(ends)]),
                cells,
                lax.ppermute(head, axis, [((i + 1) % count, i) for i in range(ends)]),
            ],
            axis=dim,
        )
    return cells


def local(inputs, cotangent, kernel_tiles, mix_weight, slot_row, slot_lon, slot_count, scale_exps):
    rows_here = inputs.shape[1]
    lon_width = inputs.shape[2]
    channels = inputs.shape[3]
    slot_total = kernel_tiles.shape[1]
    basis_count = kernel_tiles.shape[2]
    tile_size = kernel_tiles.shape[3]
    lon_blocks = lon_width // tile_size
    points = rows_here * lon_width
    mix_major = (
        mix_weight.reshape(channels, basis_count, channels)
        .transpose(1, 0, 2)
        .reshape(basis_count * channels, channels)
    )
    extended = extended_2(inputs, (("lat", 1),), 1)
    blocks = extended[0].reshape(rows_here + 2, lon_blocks, tile_size, channels)
    row_ids = jnp.arange(rows_here, dtype=jnp.int32)
    blk_ids = jnp.arange(lon_blocks, dtype=jnp.int32)
    sources = []
    shifts = []
    masked = []
    for slot_index in range(slot_total):
        sources.append(row_ids + slot_row[:, slot_index] + 1)
        shifts.append((blk_ids[None, :] + slot_lon[:, slot_index][:, None]) % lon_blocks)
        keep_mask = (slot_index < slot_count).astype(jnp.bfloat16)
        masked.append(kernel_tiles[:, slot_index] * keep_mask[:, None, None, None])
    accum = jnp.zeros((rows_here, lon_blocks, tile_size, basis_count, channels), jnp.float32)
    for slot_index in range(slot_total):
        picked = blocks[sources[slot_index][:, None], shifts[slot_index]]
        accum = accum + jnp.einsum(
            "rkpq,rjqc->rjpkc", masked[slot_index], picked, preferred_element_type=jnp.float32
        )
    basis_out = accum.reshape(points, basis_count * channels).astype(jnp.bfloat16)
    mixed = jnp.dot(basis_out, mix_major, preferred_element_type=jnp.float32)
    gate_value = jax.nn.sigmoid(mixed)
    flat_in = inputs.reshape(points, channels).astype(jnp.float32)
    result = (flat_in + mixed * gate_value).astype(jnp.bfloat16).reshape(inputs.shape)
    flat_cot = cotangent.reshape(points, channels).astype(jnp.float32)
    dmixed = (flat_cot * gate_value * (1.0 + mixed * (1.0 - gate_value))).astype(jnp.bfloat16)
    dbasis = lax.dot_general(
        dmixed, mix_major, (((1,), (1,)), ((), ())), preferred_element_type=jnp.float32
    ).astype(jnp.bfloat16)
    dbasis = dbasis.reshape(rows_here, lon_blocks, tile_size, basis_count, channels)
    back_ext = jnp.zeros((rows_here + 2, lon_blocks, tile_size, channels), jnp.float32)
    for slot_index in range(slot_total):
        slot_term = jnp.einsum(
            "rkpq,rjpkc->rjqc", masked[slot_index], dbasis, preferred_element_type=jnp.float32
        )
        back_ext = back_ext.at[sources[slot_index][:, None], shifts[slot_index]].add(slot_term)
    rim_rows = jnp.concatenate([back_ext[:1], back_ext[rows_here + 1 :]], axis=0).reshape(
        2, lon_width, channels
    )
    returned = extended_2(rim_rows.astype(jnp.bfloat16), (("lat", 0),), 1).astype(rim_rows.dtype)
    inner_grad = back_ext[1 : rows_here + 1].reshape(rows_here, lon_width, channels)
    inner_grad = inner_grad.at[0].add(returned[0])
    inner_grad = inner_grad.at[rows_here - 1].add(returned[3])
    grad_in = (cotangent[0].astype(jnp.float32) + inner_grad).astype(jnp.bfloat16)[None]
    major_part = lax.dot_general(
        basis_out, dmixed, (((0,), (0,)), ((), ())), preferred_element_type=jnp.float32
    )
    partial_value = (
        major_part.reshape(basis_count, channels, channels)
        .transpose(1, 0, 2)
        .reshape(channels * basis_count, channels)
    )
    row_part = lax.psum_scatter(partial_value, "dp", scatter_dimension=0, tiled=True)
    grad_total = lax.psum(row_part, "lat")
    factor = jnp.repeat(jnp.exp2(-scale_exps.astype(jnp.float32)), tile_size, axis=1)
    count_all = lax.axis_size("dp") * inputs.shape[0] * lax.axis_size("lat") * rows_here * lon_width
    weight_grad = grad_total * factor / math.sqrt(count_all)
    return (result, grad_in, weight_grad)


MESH = pl.DeviceIdType.MESH
TILE = 16
LANES = 128
CHUNKS = (4, 3)


def dot(a, b, da, db):
    return lax.dot_general(a, b, (((da,), (db,)), ((), ())), preferred_element_type=jnp.float32)


def fused(
    row_ref, count_ref, scale_ref, x_hbm, cot_hbm, tiles_hbm, w_hbm,
    out_ref, gin_ref, wg_ref,
    xs, cot, tiles, w, wk, tmat, bas, dmix, dbas, back, rim, gt_a, gt_b, r1_a, r1_b, s1_a, s1_b, r2_a, r2_b, q_a, q_b, gk,
    load_sem, halo_s, halo_r, fac_s, fac_r, xy_s, xy_r, rim_s, rim_r, z_s, z_r, lat_s, lat_r,
):
    lat = lax.axis_index("lat")
    dp = lax.axis_index("dp")
    last = 3
    x, c = lat // 2, lat % 2
    z, y = dp // 2, dp % 2
    slots, basis = tiles.shape[0], tiles.shape[1]
    size = tiles.shape[2]
    chans = w.shape[1]
    f32, bf16 = jnp.float32, jnp.bfloat16

    loads = [
        pltpu.make_async_copy(tiles_hbm.at[0], tiles, load_sem.at[0]),
        pltpu.make_async_copy(w_hbm, w, load_sem.at[1]),
        pltpu.make_async_copy(x_hbm.at[0, 0], xs.at[0], load_sem.at[2]),
        pltpu.make_async_copy(cot_hbm.at[0, 0], cot, load_sem.at[3]),
    ]
    barrier = pltpu.get_barrier_semaphore()
    x_lat = (1 - x) * 2 + c
    c_lat = x * 2 + (1 - c)
    xc_lat = 3 - lat
    y_dp = z * 2 + (1 - y)
    z_dps = [((z + o) % 4) * 2 + y for o in (1, 2, 3)]
    friends = [(x_lat, dp), (c_lat, dp), (xc_lat, dp), (lat, y_dp), (x_lat, y_dp)]
    friends += [(lat, d) for d in z_dps]
    for friend in friends:
        pl.semaphore_signal(barrier, inc=1, device_id=friend, device_id_type=MESH)
    loads[2].start()
    loads[0].start()
    loads[1].start()
    loads[3].start()
    pl.semaphore_wait(barrier, len(friends))

    def remote(src, dst, send, recv, target):
        return pltpu.make_async_remote_copy(
            src_ref=src, dst_ref=dst, send_sem=send, recv_sem=recv,
            device_id=target, device_id_type=MESH,
        )

    down = remote(x_hbm.at[0, 0], xs.at[1], halo_s.at[0], halo_r.at[0], (lat + 1, dp))
    up = remote(x_hbm.at[0, 0], xs.at[2], halo_s.at[1], halo_r.at[1], (lat - 1, dp))

    @pl.when(lat < last)
    def _():
        down.start()

    @pl.when(lat > 0)
    def _():
        up.start()

    @pl.when(lat == 0)
    def _():
        xs[1] = jnp.zeros(xs.shape[1:], bf16)
        rim[2] = jnp.zeros(rim.shape[1:], bf16)

    @pl.when(lat == last)
    def _():
        xs[2] = jnp.zeros(xs.shape[1:], bf16)
        rim[3] = jnp.zeros(rim.shape[1:], bf16)

    gts, r1s, s1s, r2s, qs = (gt_a, gt_b), (r1_a, r1_b), (s1_a, s1_b), (r2_a, r2_b), (q_a, q_b)
    gt_b[:, 3, :, 32:48, :] = jnp.zeros((2, 4, TILE, LANES), bf16)

    loads[0].wait()
    count = count_ref[0]
    offs = (0, -1, 1)
    weight = [
        [jnp.where(jnp.logical_and(row_ref[0, s] == d, s < count), 1.0, 0.0).astype(f32) for s in range(3, slots)]
        for d in offs
    ]
    for k in range(basis):
        extra = [tiles[s, k].astype(f32) for s in range(3, slots)]
        for n in range(3):
            total = tiles[n, k].astype(f32)
            for t, e in zip(weight[n], extra):
                total = total + t * e
            tmat[k * size : (k + 1) * size, n * size : (n + 1) * size] = total.astype(bf16)

    loads[1].wait()
    blk = 64
    r = lax.broadcasted_iota(jnp.int32, (basis * blk, basis * blk), 0)
    col = lax.broadcasted_iota(jnp.int32, (basis * blk, basis * blk), 1)
    kk = (r >= blk).astype(jnp.int32) + (r >= 2 * blk).astype(jnp.int32)
    perm = jnp.where(col == 3 * (r - blk * kk) + kk, 1.0, 0.0).astype(bf16)
    for b in range(chans // blk):
        part = dot(perm, w[b * basis * blk : (b + 1) * basis * blk, :], 1, 0).astype(bf16)
        for k in range(basis):
            wk[k, b * blk : (b + 1) * blk, :] = part[k * blk : (k + 1) * blk, :]

    loads[2].wait()
    loads[3].wait()

    @pl.when(lat > 0)
    def _():
        down.wait_recv()

    @pl.when(lat < last)
    def _():
        up.wait_recv()

    bas[0] = dot(tmat[...], xs[...].reshape(3 * size, chans), 1, 0).astype(bf16)
    send_bas = remote(bas.at[0], bas.at[1], fac_s.at[0], fac_r.at[0], (c_lat, dp))
    send_bas.start()
    mixed = dot(bas[0, 0:size, :], wk[0], 1, 0)
    for k in range(1, basis):
        mixed = mixed + dot(bas[0, k * size : (k + 1) * size, :], wk[k], 1, 0)
    gate = jax.nn.sigmoid(mixed)
    dmix[0] = (cot[...].astype(f32) * gate * (1.0 + mixed * (1.0 - gate))).astype(bf16)
    send_dmix = remote(dmix.at[0], dmix.at[1], fac_s.at[1], fac_r.at[1], (c_lat, dp))
    send_dmix.start()
    out_ref[0, 0] = (xs[0].astype(f32) + mixed * gate).astype(bf16)

    dm = dmix[0]
    for k in range(basis):
        dbas[k * size : (k + 1) * size, :] = dot(dm, wk[k], 1, 1).astype(bf16)

    send_bas.wait_recv()
    send_dmix.wait_recv()
    both = dmix[...].reshape(2 * size, chans)

    def exchange(h):
        gt, r1 = gts[h], r1s[h]
        ends = (
            (2, gt.at[1 - y, x_lat], (x_lat, y_dp)),
            (0, gt.at[y, x_lat], (x_lat, dp)),
            (1, gt.at[1 - y, lat], (lat, y_dp)),
        )
        copies = [remote(src, r1.at[n], xy_s.at[3 * h + n], xy_r.at[3 * h + n], to) for n, src, to in ends]
        for copy in copies:
            copy.start()
        return copies

    xy = [None, None]
    for k in range(basis):
        lhs = jnp.concatenate([bas[0, k * size : (k + 1) * size, :], bas[1, k * size : (k + 1) * size, :]], axis=0)
        grad = dot(lhs, both, 0, 0).astype(bf16)
        for d in range(8):
            for i in range(3):
                for j in range(3):
                    at, part = divmod((k * 3 + i) * 3 + j, 4)
                    h, at = (0, at) if at < CHUNKS[0] else (1, at - CHUNKS[0])
                    lo = 48 * d + TILE * i
                    gts[h][d % 2, part, d // 2, at * TILE : (at + 1) * TILE, :] = grad[
                        lo : lo + TILE, j * LANES : (j + 1) * LANES
                    ]
        if k == 1:
            xy[0] = exchange(0)
    xy[1] = exchange(1)

    back[...] = dot(tmat[...], dbas[...], 0, 0)
    rim[0] = back[size : 2 * size, :].astype(bf16)
    rim[1] = back[2 * size : 3 * size, :].astype(bf16)
    rim_up = remote(rim.at[0], rim.at[3], rim_s.at[0], rim_r.at[0], (lat - 1, dp))
    rim_down = remote(rim.at[1], rim.at[2], rim_s.at[1], rim_r.at[1], (lat + 1, dp))

    @pl.when(lat > 0)
    def _():
        rim_up.start()

    @pl.when(lat < last)
    def _():
        rim_down.start()

    zs = []
    for h in range(2):
        for copy in xy[h]:
            copy.wait_recv()
        own, r1, s1, r2 = gts[h].at[y, lat], r1s[h], s1s[h], r2s[h]
        for n in range(4):
            s1[n] = (
                own[n].astype(f32) + r1[0, n].astype(f32) + (r1[1, n].astype(f32) + r1[2, n].astype(f32))
            ).astype(bf16)
        zs.append(
            [
                remote(
                    s1.at[(z + o) % 4], r2.at[o - 1], z_s.at[3 * h + o - 1], z_r.at[3 * h + o - 1],
                    (lat, z_dps[o - 1]),
                )
                for o in (2, 1, 3)
            ]
        )
        for copy in zs[h]:
            copy.start()

    @pl.when(lat < last)
    def _():
        rim_up.wait_recv()

    @pl.when(lat > 0)
    def _():
        rim_down.wait_recv()

    gin_ref[0, 0] = (
        cot[...].astype(f32) + back[0:size, :] + rim[2].astype(f32) + rim[3].astype(f32)
    ).astype(bf16)

    lats, arrive = [], []
    for h in range(2):
        for copy in zs[h]:
            copy.wait_recv()
        s1, r2, q = s1s[h], r2s[h], qs[h]
        q[lat] = (
            s1[z].astype(f32) + r2[0].astype(f32) + (r2[1].astype(f32) + r2[2].astype(f32))
        ).astype(bf16)
        for n, other in ((2, xc_lat), (0, x_lat), (1, c_lat)):
            copy = remote(q.at[lat], q.at[lat], lat_s.at[3 * h + n], lat_r.at[3 * h + n], (other, dp))
            copy.start()
            lats.append(copy)
            arrive.append(
                remote(q.at[other], q.at[other], lat_s.at[3 * h + n], lat_r.at[3 * h + n], (other, dp))
            )
    rr = lax.broadcasted_iota(jnp.int32, (144, 144), 0)
    cc = lax.broadcasted_iota(jnp.int32, (144, 144), 1)
    kc = (cc >= 48).astype(jnp.int32) + (cc >= 96).astype(jnp.int32)
    order = jnp.where(rr == 3 * (cc - 48 * kc) + kc, 1.0, 0.0).astype(bf16)
    factor = jnp.exp2(-scale_ref[...].astype(f32)) * (1.0 / math.sqrt(4 * 8 * size))
    jr = lax.broadcasted_iota(jnp.int32, (3, chans), 0)
    jc = lax.broadcasted_iota(jnp.int32, (3, chans), 1)
    spread = jnp.where(jnp.logical_and(jc >= jr * LANES, jc < (jr + 1) * LANES), 1.0, 0.0).astype(f32)
    factor = dot(factor, spread, 0, 0)
    for copy in arrive:
        copy.wait_recv()
    for t in range(27):
        at, part = divmod(t, 4)
        q, at = (q_a, at) if at < CHUNKS[0] else (q_b, at - CHUNKS[0])
        g, j = divmod(t, 3)
        gk[g * TILE : (g + 1) * TILE, j * LANES : (j + 1) * LANES] = q[part, at * TILE : (at + 1) * TILE, :]
    wg_ref[...] = dot(order, gk[...], 1, 0) * factor

    @pl.when(lat < last)
    def _():
        down.wait_send()
        rim_down.wait_send()

    @pl.when(lat > 0)
    def _():
        up.wait_send()
        rim_up.wait_send()

    for copy in [send_bas, send_dmix] + xy[0] + xy[1] + zs[0] + zs[1] + lats:
        copy.wait_send()


def local_fused(inputs, cotangent, kernel_tiles, mix_weight, slot_row, slot_lon, slot_count, scale_exps):
    size, chans = inputs.shape[2], inputs.shape[3]
    basis = kernel_tiles.shape[2]
    bf16, f32 = jnp.bfloat16, jnp.float32
    dma = pltpu.SemaphoreType.DMA
    vmem = pl.BlockSpec(memory_space=pltpu.VMEM)
    smem = pl.BlockSpec(memory_space=pltpu.SMEM)
    hbm = pl.BlockSpec(memory_space=pltpu.HBM)
    return pl.pallas_call(
        fused,
        out_shape=(
            jax.ShapeDtypeStruct(inputs.shape, bf16),
            jax.ShapeDtypeStruct(inputs.shape, bf16),
            jax.ShapeDtypeStruct((basis * chans // 8, chans), f32),
        ),
        in_specs=[smem, smem, vmem, hbm, hbm, hbm, hbm],
        out_specs=(vmem, vmem, vmem),
        scratch_shapes=[
            pltpu.VMEM((3, size, chans), bf16),
            pltpu.VMEM((size, chans), bf16),
            pltpu.VMEM(kernel_tiles.shape[1:], bf16),
            pltpu.VMEM(mix_weight.shape, bf16),
            pltpu.VMEM((basis, chans, chans), bf16),
            pltpu.VMEM((basis * size, 3 * size), bf16),
            pltpu.VMEM((2, basis * size, chans), bf16),
            pltpu.VMEM((2, size, chans), bf16),
            pltpu.VMEM((basis * size, chans), bf16),
            pltpu.VMEM((3 * size, chans), f32),
            pltpu.VMEM((4, size, chans), bf16),
            *[pltpu.VMEM((2, 4, 4, n * TILE, LANES), bf16) for n in CHUNKS],
            *[pltpu.VMEM((3, 4, n * TILE, LANES), bf16) for n in CHUNKS],
            *[pltpu.VMEM((4, n * TILE, LANES), bf16) for n in CHUNKS],
            *[pltpu.VMEM((3, n * TILE, LANES), bf16) for n in CHUNKS],
            *[pltpu.VMEM((4, n * TILE, LANES), bf16) for n in CHUNKS],
            pltpu.VMEM((144, chans), bf16),
            dma((4,)), dma((2,)), dma((2,)), dma((2,)), dma((2,)), dma((6,)), dma((6,)),
            dma((2,)), dma((2,)), dma((6,)), dma((6,)), dma((6,)), dma((6,)),
        ],
        compiler_params=pltpu.CompilerParams(
            collective_id=0, has_side_effects=True, vmem_limit_bytes=65472 * 1024
        ),
        cost_estimate=pl.CostEstimate(flops=10**9, bytes_accessed=3 * 10**6, transcendentals=50000),
    )(slot_row, slot_count, scale_exps.T, inputs, cotangent, kernel_tiles, mix_weight)


def fits(mesh):
    return mesh.shape["lat"] == 4 and mesh.shape["dp"] == 8


def solution(mesh):
    in_specs = (
        P("dp", "lat", None, None),
        P("dp", "lat", None, None),
        P("lat", None, None, None, None),
        P(),
        P("lat", None),
        P("lat", None),
        P("lat"),
        P("dp", None),
    )
    out_specs = (P("dp", "lat", None, None), P("dp", "lat", None, None), P("dp", None))
    body = local_fused if fits(mesh) else local
    return jax.shard_map(body, mesh=mesh, in_specs=in_specs, out_specs=out_specs, check_vma=False)
```

```python
import math

import jax
import jax.numpy as jnp
from jax import lax
from jax.experimental import pallas as pl
from jax.experimental.pallas import tpu as pltpu
from jax.sharding import PartitionSpec as P


def extended_2(cells, sides, width):
    for axis, dim in sides:
        count = lax.axis_size(axis)
        ends = count - 1
        head = lax.slice_in_dim(cells, 0, width, axis=dim)
        tail = lax.slice_in_dim(cells, cells.shape[dim] - width, cells.shape[dim], axis=dim)
        cells = jnp.concatenate(
            [
                lax.ppermute(tail, axis, [(i, (i + 1) % count) for i in range(ends)]),
                cells,
                lax.ppermute(head, axis, [((i + 1) % count, i) for i in range(ends)]),
            ],
            axis=dim,
        )
    return cells


def local(inputs, cotangent, kernel_tiles, mix_weight, slot_row, slot_lon, slot_count, scale_exps):
    rows_here = inputs.shape[1]
    lon_width = inputs.shape[2]
    channels = inputs.shape[3]
    slot_total = kernel_tiles.shape[1]
    basis_count = kernel_tiles.shape[2]
    tile_size = kernel_tiles.shape[3]
    lon_blocks = lon_width // tile_size
    points = rows_here * lon_width
    mix_major = (
        mix_weight.reshape(channels, basis_count, channels)
        .transpose(1, 0, 2)
        .reshape(basis_count * channels, channels)
    )
    extended = extended_2(inputs, (("lat", 1),), 1)
    blocks = extended[0].reshape(rows_here + 2, lon_blocks, tile_size, channels)
    row_ids = jnp.arange(rows_here, dtype=jnp.int32)
    blk_ids = jnp.arange(lon_blocks, dtype=jnp.int32)
    sources = []
    shifts = []
    masked = []
    for slot_index in range(slot_total):
        sources.append(row_ids + slot_row[:, slot_index] + 1)
        shifts.append((blk_ids[None, :] + slot_lon[:, slot_index][:, None]) % lon_blocks)
        keep_mask = (slot_index < slot_count).astype(jnp.bfloat16)
        masked.append(kernel_tiles[:, slot_index] * keep_mask[:, None, None, None])
    accum = jnp.zeros((rows_here, lon_blocks, tile_size, basis_count, channels), jnp.float32)
    for slot_index in range(slot_total):
        picked = blocks[sources[slot_index][:, None], shifts[slot_index]]
        accum = accum + jnp.einsum(
            "rkpq,rjqc->rjpkc", masked[slot_index], picked, preferred_element_type=jnp.float32
        )
    basis_out = accum.reshape(points, basis_count * channels).astype(jnp.bfloat16)
    mixed = jnp.dot(basis_out, mix_major, preferred_element_type=jnp.float32)
    gate_value = jax.nn.sigmoid(mixed)
    flat_in = inputs.reshape(points, channels).astype(jnp.float32)
    result = (flat_in + mixed * gate_value).astype(jnp.bfloat16).reshape(inputs.shape)
    flat_cot = cotangent.reshape(points, channels).astype(jnp.float32)
    dmixed = (flat_cot * gate_value * (1.0 + mixed * (1.0 - gate_value))).astype(jnp.bfloat16)
    dbasis = lax.dot_general(
        dmixed, mix_major, (((1,), (1,)), ((), ())), preferred_element_type=jnp.float32
    ).astype(jnp.bfloat16)
    dbasis = dbasis.reshape(rows_here, lon_blocks, tile_size, basis_count, channels)
    back_ext = jnp.zeros((rows_here + 2, lon_blocks, tile_size, channels), jnp.float32)
    for slot_index in range(slot_total):
        slot_term = jnp.einsum(
            "rkpq,rjpkc->rjqc", masked[slot_index], dbasis, preferred_element_type=jnp.float32
        )
        back_ext = back_ext.at[sources[slot_index][:, None], shifts[slot_index]].add(slot_term)
    rim_rows = jnp.concatenate([back_ext[:1], back_ext[rows_here + 1 :]], axis=0).reshape(
        2, lon_width, channels
    )
    returned = extended_2(rim_rows.astype(jnp.bfloat16), (("lat", 0),), 1).astype(rim_rows.dtype)
    inner_grad = back_ext[1 : rows_here + 1].reshape(rows_here, lon_width, channels)
    inner_grad = inner_grad.at[0].add(returned[0])
    inner_grad = inner_grad.at[rows_here - 1].add(returned[3])
    grad_in = (cotangent[0].astype(jnp.float32) + inner_grad).astype(jnp.bfloat16)[None]
    major_part = lax.dot_general(
        basis_out, dmixed, (((0,), (0,)), ((), ())), preferred_element_type=jnp.float32
    )
    partial_value = (
        major_part.reshape(basis_count, channels, channels)
        .transpose(1, 0, 2)
        .reshape(channels * basis_count, channels)
    )
    row_part = lax.psum_scatter(partial_value, "dp", scatter_dimension=0, tiled=True)
    grad_total = lax.psum(row_part, "lat")
    factor = jnp.repeat(jnp.exp2(-scale_exps.astype(jnp.float32)), tile_size, axis=1)
    count_all = lax.axis_size("dp") * inputs.shape[0] * lax.axis_size("lat") * rows_here * lon_width
    weight_grad = grad_total * factor / math.sqrt(count_all)
    return (result, grad_in, weight_grad)


MESH = pl.DeviceIdType.MESH
TILE = 16
LANES = 128
CHUNKS = (4, 3)


def dot(a, b, da, db):
    return lax.dot_general(a, b, (((da,), (db,)), ((), ())), preferred_element_type=jnp.float32)


def fused(
    row_ref, count_ref, scale_ref, x_hbm, cot_hbm, tiles_hbm, w_hbm,
    out_ref, gin_ref, wg_ref,
    xs, cot, tiles, w, wk, tmat, bas, dmix, dbas, back, rim, gt_a, gt_b, r1_a, r1_b, s1_a, s1_b, r2_a, r2_b, q_a, q_b, gk,
    load_sem, halo_s, halo_r, fac_s, fac_r, xy_s, xy_r, rim_s, rim_r, z_s, z_r, lat_s, lat_r,
):
    lat = lax.axis_index("lat")
    dp = lax.axis_index("dp")
    last = 3
    x, c = lat // 2, lat % 2
    z, y = dp // 2, dp % 2
    slots, basis = tiles.shape[0], tiles.shape[1]
    size = tiles.shape[2]
    chans = w.shape[1]
    f32, bf16 = jnp.float32, jnp.bfloat16

    loads = [
        pltpu.make_async_copy(tiles_hbm.at[0], tiles, load_sem.at[0]),
        pltpu.make_async_copy(w_hbm, w, load_sem.at[1]),
        pltpu.make_async_copy(x_hbm.at[0, 0], xs.at[0], load_sem.at[2]),
        pltpu.make_async_copy(cot_hbm.at[0, 0], cot, load_sem.at[3]),
    ]
    barrier = pltpu.get_barrier_semaphore()
    x_lat = (1 - x) * 2 + c
    c_lat = x * 2 + (1 - c)
    xc_lat = 3 - lat
    y_dp = z * 2 + (1 - y)
    z_dps = [((z + o) % 4) * 2 + y for o in (1, 2, 3)]
    friends = [(x_lat, dp), (c_lat, dp), (xc_lat, dp), (lat, y_dp), (x_lat, y_dp)]
    friends += [(lat, d) for d in z_dps]
    for friend in friends:
        pl.semaphore_signal(barrier, inc=1, device_id=friend, device_id_type=MESH)
    loads[2].start()
    loads[0].start()
    loads[1].start()
    loads[3].start()
    pl.semaphore_wait(barrier, len(friends))

    def remote(src, dst, send, recv, target):
        return pltpu.make_async_remote_copy(
            src_ref=src, dst_ref=dst, send_sem=send, recv_sem=recv,
            device_id=target, device_id_type=MESH,
        )

    down = remote(x_hbm.at[0, 0], xs.at[1], halo_s.at[0], halo_r.at[0], (lat + 1, dp))
    up = remote(x_hbm.at[0, 0], xs.at[2], halo_s.at[1], halo_r.at[1], (lat - 1, dp))

    @pl.when(lat < last)
    def _():
        down.start()

    @pl.when(lat > 0)
    def _():
        up.start()

    @pl.when(lat == 0)
    def _():
        xs[1] = jnp.zeros(xs.shape[1:], bf16)
        rim[2] = jnp.zeros(rim.shape[1:], bf16)

    @pl.when(lat == last)
    def _():
        xs[2] = jnp.zeros(xs.shape[1:], bf16)
        rim[3] = jnp.zeros(rim.shape[1:], bf16)

    gts, r1s, s1s, r2s, qs = (gt_a, gt_b), (r1_a, r1_b), (s1_a, s1_b), (r2_a, r2_b), (q_a, q_b)
    gt_b[:, 3, :, 32:48, :] = jnp.zeros((2, 4, TILE, LANES), bf16)

    loads[0].wait()
    count = count_ref[0]
    offs = (0, -1, 1)
    weight = [
        [jnp.where(jnp.logical_and(row_ref[0, s] == d, s < count), 1.0, 0.0).astype(f32) for s in range(3, slots)]
        for d in offs
    ]
    for k in range(basis):
        extra = [tiles[s, k].astype(f32) for s in range(3, slots)]
        for n in range(3):
            total = tiles[n, k].astype(f32)
            for t, e in zip(weight[n], extra):
                total = total + t * e
            tmat[k * size : (k + 1) * size, n * size : (n + 1) * size] = total.astype(bf16)

    loads[1].wait()
    blk = 64
    r = lax.broadcasted_iota(jnp.int32, (basis * blk, basis * blk), 0)
    col = lax.broadcasted_iota(jnp.int32, (basis * blk, basis * blk), 1)
    kk = (r >= blk).astype(jnp.int32) + (r >= 2 * blk).astype(jnp.int32)
    perm = jnp.where(col == 3 * (r - blk * kk) + kk, 1.0, 0.0).astype(bf16)
    for b in range(chans // blk):
        part = dot(perm, w[b * basis * blk : (b + 1) * basis * blk, :], 1, 0).astype(bf16)
        for k in range(basis):
            wk[k, b * blk : (b + 1) * blk, :] = part[k * blk : (k + 1) * blk, :]

    loads[2].wait()
    loads[3].wait()

    @pl.when(lat > 0)
    def _():
        down.wait_recv()

    @pl.when(lat < last)
    def _():
        up.wait_recv()

    bas[0] = dot(tmat[...], xs[...].reshape(3 * size, chans), 1, 0).astype(bf16)
    send_bas = remote(bas.at[0], bas.at[1], fac_s.at[0], fac_r.at[0], (c_lat, dp))
    send_bas.start()
    mixed = dot(bas[0, 0:size, :], wk[0], 1, 0)
    for k in range(1, basis):
        mixed = mixed + dot(bas[0, k * size : (k + 1) * size, :], wk[k], 1, 0)
    gate = jax.nn.sigmoid(mixed)
    dmix[0] = (cot[...].astype(f32) * gate * (1.0 + mixed * (1.0 - gate))).astype(bf16)
    send_dmix = remote(dmix.at[0], dmix.at[1], fac_s.at[1], fac_r.at[1], (c_lat, dp))
    send_dmix.start()
    out_ref[0, 0] = (xs[0].astype(f32) + mixed * gate).astype(bf16)

    dm = dmix[0]
    for k in range(basis):
        dbas[k * size : (k + 1) * size, :] = dot(dm, wk[k], 1, 1).astype(bf16)

    send_bas.wait_recv()
    send_dmix.wait_recv()
    both = dmix[...].reshape(2 * size, chans)

    def exchange(h):
        gt, r1 = gts[h], r1s[h]
        ends = (
            (2, gt.at[1 - y, x_lat], (x_lat, y_dp)),
            (0, gt.at[y, x_lat], (x_lat, dp)),
            (1, gt.at[1 - y, lat], (lat, y_dp)),
        )
        copies = [remote(src, r1.at[n], xy_s.at[3 * h + n], xy_r.at[3 * h + n], to) for n, src, to in ends]
        for copy in copies:
            copy.start()
        return copies

    xy = [None, None]
    for k in range(basis):
        lhs = jnp.concatenate([bas[0, k * size : (k + 1) * size, :], bas[1, k * size : (k + 1) * size, :]], axis=0)
        grad = dot(lhs, both, 0, 0).astype(bf16)
        for d in range(8):
            for i in range(3):
                for j in range(3):
                    at, part = divmod((k * 3 + i) * 3 + j, 4)
                    h, at = (0, at) if at < CHUNKS[0] else (1, at - CHUNKS[0])
                    lo = 48 * d + TILE * i
                    gts[h][d % 2, part, d // 2, at * TILE : (at + 1) * TILE, :] = grad[
                        lo : lo + TILE, j * LANES : (j + 1) * LANES
                    ]
        if k == 1:
            xy[0] = exchange(0)
    xy[1] = exchange(1)

    back[...] = dot(tmat[...], dbas[...], 0, 0)
    rim[0] = back[size : 2 * size, :].astype(bf16)
    rim[1] = back[2 * size : 3 * size, :].astype(bf16)
    rim_up = remote(rim.at[0], rim.at[3], rim_s.at[0], rim_r.at[0], (lat - 1, dp))
    rim_down = remote(rim.at[1], rim.at[2], rim_s.at[1], rim_r.at[1], (lat + 1, dp))

    @pl.when(lat > 0)
    def _():
        rim_up.start()

    @pl.when(lat < last)
    def _():
        rim_down.start()

    zs = []
    for h in range(2):
        for copy in xy[h]:
            copy.wait_recv()
        own, r1, s1, r2 = gts[h].at[y, lat], r1s[h], s1s[h], r2s[h]
        for n in range(4):
            s1[n] = (
                own[n].astype(f32) + r1[0, n].astype(f32) + (r1[1, n].astype(f32) + r1[2, n].astype(f32))
            ).astype(bf16)
        zs.append(
            [
                remote(
                    s1.at[(z + o) % 4], r2.at[o - 1], z_s.at[3 * h + o - 1], z_r.at[3 * h + o - 1],
                    (lat, z_dps[o - 1]),
                )
                for o in (2, 1, 3)
            ]
        )
        for copy in zs[h]:
            copy.start()

    @pl.when(lat < last)
    def _():
        rim_up.wait_recv()

    @pl.when(lat > 0)
    def _():
        rim_down.wait_recv()

    gin_ref[0, 0] = (
        cot[...].astype(f32) + back[0:size, :] + rim[2].astype(f32) + rim[3].astype(f32)
    ).astype(bf16)

    lats, arrive = [], []
    for h in range(2):
        for copy in zs[h]:
            copy.wait_recv()
        s1, r2, q = s1s[h], r2s[h], qs[h]
        q[lat] = (
            s1[z].astype(f32) + r2[0].astype(f32) + (r2[1].astype(f32) + r2[2].astype(f32))
        ).astype(bf16)
        for n, other in ((2, xc_lat), (0, x_lat), (1, c_lat)):
            copy = remote(q.at[lat], q.at[lat], lat_s.at[3 * h + n], lat_r.at[3 * h + n], (other, dp))
            copy.start()
            lats.append(copy)
            arrive.append(
                remote(q.at[other], q.at[other], lat_s.at[3 * h + n], lat_r.at[3 * h + n], (other, dp))
            )
    rr = lax.broadcasted_iota(jnp.int32, (144, 144), 0)
    cc = lax.broadcasted_iota(jnp.int32, (144, 144), 1)
    kc = (cc >= 48).astype(jnp.int32) + (cc >= 96).astype(jnp.int32)
    order = jnp.where(rr == 3 * (cc - 48 * kc) + kc, 1.0, 0.0).astype(bf16)
    factor = jnp.exp2(-scale_ref[...].astype(f32)) * (1.0 / math.sqrt(4 * 8 * size))
    jr = lax.broadcasted_iota(jnp.int32, (3, chans), 0)
    jc = lax.broadcasted_iota(jnp.int32, (3, chans), 1)
    spread = jnp.where(jnp.logical_and(jc >= jr * LANES, jc < (jr + 1) * LANES), 1.0, 0.0).astype(f32)
    factor = dot(factor, spread, 0, 0)
    for copy in arrive:
        copy.wait_recv()
    for t in range(27):
        at, part = divmod(t, 4)
        q, at = (q_a, at) if at < CHUNKS[0] else (q_b, at - CHUNKS[0])
        g, j = divmod(t, 3)
        gk[g * TILE : (g + 1) * TILE, j * LANES : (j + 1) * LANES] = q[part, at * TILE : (at + 1) * TILE, :]
    wg_ref[...] = dot(order, gk[...], 1, 0) * factor

    @pl.when(lat < last)
    def _():
        down.wait_send()
        rim_down.wait_send()

    @pl.when(lat > 0)
    def _():
        up.wait_send()
        rim_up.wait_send()

    for copy in [send_bas, send_dmix] + xy[0] + xy[1] + zs[0] + zs[1] + lats:
        copy.wait_send()


def deliver(a_ref, b_ref, c_ref, a_out, b_out, c_out, sems):
    pairs = ((a_ref, a_out), (b_ref, b_out), (c_ref, c_out))
    copies = [pltpu.make_async_copy(src, dst, sems.at[n]) for n, (src, dst) in enumerate(pairs)]
    for copy in copies:
        copy.start()
    for copy in copies:
        copy.wait()


def local_fused(inputs, cotangent, kernel_tiles, mix_weight, slot_row, slot_lon, slot_count, scale_exps):
    size, chans = inputs.shape[2], inputs.shape[3]
    basis = kernel_tiles.shape[2]
    bf16, f32 = jnp.bfloat16, jnp.float32
    dma = pltpu.SemaphoreType.DMA
    vmem = pl.BlockSpec(memory_space=pltpu.VMEM)
    smem = pl.BlockSpec(memory_space=pltpu.SMEM)
    hbm = pl.BlockSpec(memory_space=pltpu.HBM)
    results = pl.pallas_call(
        fused,
        out_shape=(
            pltpu.VMEM(inputs.shape, bf16),
            pltpu.VMEM(inputs.shape, bf16),
            pltpu.VMEM((basis * chans // 8, chans), f32),
        ),
        in_specs=[smem, smem, vmem, hbm, hbm, hbm, hbm],
        out_specs=(vmem, vmem, vmem),
        scratch_shapes=[
            pltpu.VMEM((3, size, chans), bf16),
            pltpu.VMEM((size, chans), bf16),
            pltpu.VMEM(kernel_tiles.shape[1:], bf16),
            pltpu.VMEM(mix_weight.shape, bf16),
            pltpu.VMEM((basis, chans, chans), bf16),
            pltpu.VMEM((basis * size, 3 * size), bf16),
            pltpu.VMEM((2, basis * size, chans), bf16),
            pltpu.VMEM((2, size, chans), bf16),
            pltpu.VMEM((basis * size, chans), bf16),
            pltpu.VMEM((3 * size, chans), f32),
            pltpu.VMEM((4, size, chans), bf16),
            *[pltpu.VMEM((2, 4, 4, n * TILE, LANES), bf16) for n in CHUNKS],
            *[pltpu.VMEM((3, 4, n * TILE, LANES), bf16) for n in CHUNKS],
            *[pltpu.VMEM((4, n * TILE, LANES), bf16) for n in CHUNKS],
            *[pltpu.VMEM((3, n * TILE, LANES), bf16) for n in CHUNKS],
            *[pltpu.VMEM((4, n * TILE, LANES), bf16) for n in CHUNKS],
            pltpu.VMEM((144, chans), bf16),
            dma((4,)), dma((2,)), dma((2,)), dma((2,)), dma((2,)), dma((6,)), dma((6,)),
            dma((2,)), dma((2,)), dma((6,)), dma((6,)), dma((6,)), dma((6,)),
        ],
        compiler_params=pltpu.CompilerParams(
            collective_id=0, has_side_effects=True, vmem_limit_bytes=64960 * 1024
        ),
        cost_estimate=pl.CostEstimate(flops=10**9, bytes_accessed=3 * 10**6, transcendentals=50000),
    )(slot_row, slot_count, scale_exps.T, inputs, cotangent, kernel_tiles, mix_weight)
    return pl.pallas_call(
        deliver,
        out_shape=tuple(jax.ShapeDtypeStruct(one.shape, one.dtype) for one in results),
        in_specs=[pl.BlockSpec(memory_space=pl.ANY)] * 3,
        compiler_params=pltpu.CompilerParams(vmem_limit_bytes=32 * 1024 * 1024),
        out_specs=(hbm,) * 3,
        scratch_shapes=[dma((3,))],
    )(*results)


def fits(mesh):
    return mesh.shape["lat"] == 4 and mesh.shape["dp"] == 8


def solution(mesh):
    in_specs = (
        P("dp", "lat", None, None),
        P("dp", "lat", None, None),
        P("lat", None, None, None, None),
        P(),
        P("lat", None),
        P("lat", None),
        P("lat"),
        P("dp", None),
    )
    out_specs = (P("dp", "lat", None, None), P("dp", "lat", None, None), P("dp", None))
    body = local_fused if fits(mesh) else local
    return jax.shard_map(body, mesh=mesh, in_specs=in_specs, out_specs=out_specs, check_vma=False)
```

```python
import math

import jax
import jax.numpy as jnp
from jax import lax
from jax.experimental import pallas as pl
from jax.experimental.pallas import tpu as pltpu
from jax.sharding import PartitionSpec as P


def extended_2(cells, sides, width):
    for axis, dim in sides:
        count = lax.axis_size(axis)
        ends = count - 1
        head = lax.slice_in_dim(cells, 0, width, axis=dim)
        tail = lax.slice_in_dim(cells, cells.shape[dim] - width, cells.shape[dim], axis=dim)
        cells = jnp.concatenate(
            [
                lax.ppermute(tail, axis, [(i, (i + 1) % count) for i in range(ends)]),
                cells,
                lax.ppermute(head, axis, [((i + 1) % count, i) for i in range(ends)]),
            ],
            axis=dim,
        )
    return cells


def local(inputs, cotangent, kernel_tiles, mix_weight, slot_row, slot_lon, slot_count, scale_exps):
    rows_here = inputs.shape[1]
    lon_width = inputs.shape[2]
    channels = inputs.shape[3]
    slot_total = kernel_tiles.shape[1]
    basis_count = kernel_tiles.shape[2]
    tile_size = kernel_tiles.shape[3]
    lon_blocks = lon_width // tile_size
    points = rows_here * lon_width
    mix_major = (
        mix_weight.reshape(channels, basis_count, channels)
        .transpose(1, 0, 2)
        .reshape(basis_count * channels, channels)
    )
    extended = extended_2(inputs, (("lat", 1),), 1)
    blocks = extended[0].reshape(rows_here + 2, lon_blocks, tile_size, channels)
    row_ids = jnp.arange(rows_here, dtype=jnp.int32)
    blk_ids = jnp.arange(lon_blocks, dtype=jnp.int32)
    sources = []
    shifts = []
    masked = []
    for slot_index in range(slot_total):
        sources.append(row_ids + slot_row[:, slot_index] + 1)
        shifts.append((blk_ids[None, :] + slot_lon[:, slot_index][:, None]) % lon_blocks)
        keep_mask = (slot_index < slot_count).astype(jnp.bfloat16)
        masked.append(kernel_tiles[:, slot_index] * keep_mask[:, None, None, None])
    accum = jnp.zeros((rows_here, lon_blocks, tile_size, basis_count, channels), jnp.float32)
    for slot_index in range(slot_total):
        picked = blocks[sources[slot_index][:, None], shifts[slot_index]]
        accum = accum + jnp.einsum(
            "rkpq,rjqc->rjpkc", masked[slot_index], picked, preferred_element_type=jnp.float32
        )
    basis_out = accum.reshape(points, basis_count * channels).astype(jnp.bfloat16)
    mixed = jnp.dot(basis_out, mix_major, preferred_element_type=jnp.float32)
    gate_value = jax.nn.sigmoid(mixed)
    flat_in = inputs.reshape(points, channels).astype(jnp.float32)
    result = (flat_in + mixed * gate_value).astype(jnp.bfloat16).reshape(inputs.shape)
    flat_cot = cotangent.reshape(points, channels).astype(jnp.float32)
    dmixed = (flat_cot * gate_value * (1.0 + mixed * (1.0 - gate_value))).astype(jnp.bfloat16)
    dbasis = lax.dot_general(
        dmixed, mix_major, (((1,), (1,)), ((), ())), preferred_element_type=jnp.float32
    ).astype(jnp.bfloat16)
    dbasis = dbasis.reshape(rows_here, lon_blocks, tile_size, basis_count, channels)
    back_ext = jnp.zeros((rows_here + 2, lon_blocks, tile_size, channels), jnp.float32)
    for slot_index in range(slot_total):
        slot_term = jnp.einsum(
            "rkpq,rjpkc->rjqc", masked[slot_index], dbasis, preferred_element_type=jnp.float32
        )
        back_ext = back_ext.at[sources[slot_index][:, None], shifts[slot_index]].add(slot_term)
    rim_rows = jnp.concatenate([back_ext[:1], back_ext[rows_here + 1 :]], axis=0).reshape(
        2, lon_width, channels
    )
    returned = extended_2(rim_rows.astype(jnp.bfloat16), (("lat", 0),), 1).astype(rim_rows.dtype)
    inner_grad = back_ext[1 : rows_here + 1].reshape(rows_here, lon_width, channels)
    inner_grad = inner_grad.at[0].add(returned[0])
    inner_grad = inner_grad.at[rows_here - 1].add(returned[3])
    grad_in = (cotangent[0].astype(jnp.float32) + inner_grad).astype(jnp.bfloat16)[None]
    major_part = lax.dot_general(
        basis_out, dmixed, (((0,), (0,)), ((), ())), preferred_element_type=jnp.float32
    )
    partial_value = (
        major_part.reshape(basis_count, channels, channels)
        .transpose(1, 0, 2)
        .reshape(channels * basis_count, channels)
    )
    row_part = lax.psum_scatter(partial_value, "dp", scatter_dimension=0, tiled=True)
    grad_total = lax.psum(row_part, "lat")
    factor = jnp.repeat(jnp.exp2(-scale_exps.astype(jnp.float32)), tile_size, axis=1)
    count_all = lax.axis_size("dp") * inputs.shape[0] * lax.axis_size("lat") * rows_here * lon_width
    weight_grad = grad_total * factor / math.sqrt(count_all)
    return (result, grad_in, weight_grad)


MESH = pl.DeviceIdType.MESH
TILE = 16
LANES = 128
CHUNKS = (4, 3)


def dot(a, b, da, db):
    return lax.dot_general(a, b, (((da,), (db,)), ((), ())), preferred_element_type=jnp.float32)


def fused(
    row_ref, count_ref, scale_ref, x_hbm, cot_hbm, tiles_hbm, w_hbm,
    out_ref, gin_ref, wg_ref,
    xs, cot, tiles, w, wk, tmat, bas, dmix, dbas, back, rim, gt_a, gt_b, r1_a, r1_b, s1_a, s1_b, r2_a, r2_b, q_a, q_b, gk,
    load_sem, halo_s, halo_r, fac_s, fac_r, xy_s, xy_r, rim_s, rim_r, z_s, z_r, lat_s, lat_r,
):
    lat = lax.axis_index("lat")
    dp = lax.axis_index("dp")
    last = 3
    x, c = lat // 2, lat % 2
    z, y = dp // 2, dp % 2
    slots, basis = tiles.shape[0], tiles.shape[1]
    size = tiles.shape[2]
    chans = w.shape[1]
    f32, bf16 = jnp.float32, jnp.bfloat16

    loads = [
        pltpu.make_async_copy(tiles_hbm.at[0], tiles, load_sem.at[0]),
        pltpu.make_async_copy(w_hbm, w, load_sem.at[1]),
        pltpu.make_async_copy(x_hbm.at[0, 0], xs.at[0], load_sem.at[2]),
        pltpu.make_async_copy(cot_hbm.at[0, 0], cot, load_sem.at[3]),
    ]
    barrier = pltpu.get_barrier_semaphore()
    x_lat = (1 - x) * 2 + c
    c_lat = x * 2 + (1 - c)
    xc_lat = 3 - lat
    y_dp = z * 2 + (1 - y)
    z_dps = [((z + o) % 4) * 2 + y for o in (1, 2, 3)]
    friends = [(x_lat, dp), (c_lat, dp), (xc_lat, dp), (lat, y_dp), (x_lat, y_dp)]
    friends += [(lat, d) for d in z_dps]
    for friend in friends:
        pl.semaphore_signal(barrier, inc=1, device_id=friend, device_id_type=MESH)
    loads[2].start()
    loads[0].start()
    loads[1].start()
    loads[3].start()
    pl.semaphore_wait(barrier, len(friends))

    def remote(src, dst, send, recv, target):
        return pltpu.make_async_remote_copy(
            src_ref=src, dst_ref=dst, send_sem=send, recv_sem=recv,
            device_id=target, device_id_type=MESH,
        )

    down = remote(x_hbm.at[0, 0], xs.at[1], halo_s.at[0], halo_r.at[0], (lat + 1, dp))
    up = remote(x_hbm.at[0, 0], xs.at[2], halo_s.at[1], halo_r.at[1], (lat - 1, dp))

    @pl.when(lat < last)
    def _():
        down.start()

    @pl.when(lat > 0)
    def _():
        up.start()

    @pl.when(lat == 0)
    def _():
        xs[1] = jnp.zeros(xs.shape[1:], bf16)
        rim[2] = jnp.zeros(rim.shape[1:], bf16)

    @pl.when(lat == last)
    def _():
        xs[2] = jnp.zeros(xs.shape[1:], bf16)
        rim[3] = jnp.zeros(rim.shape[1:], bf16)

    gts, r1s, s1s, r2s, qs = (gt_a, gt_b), (r1_a, r1_b), (s1_a, s1_b), (r2_a, r2_b), (q_a, q_b)
    gt_b[:, 3, :, 32:48, :] = jnp.zeros((2, 4, TILE, LANES), bf16)

    loads[0].wait()
    count = count_ref[0]
    offs = (0, -1, 1)
    weight = [
        [jnp.where(jnp.logical_and(row_ref[0, s] == d, s < count), 1.0, 0.0).astype(f32) for s in range(3, slots)]
        for d in offs
    ]
    for k in range(basis):
        extra = [tiles[s, k].astype(f32) for s in range(3, slots)]
        for n in range(3):
            total = tiles[n, k].astype(f32)
            for t, e in zip(weight[n], extra):
                total = total + t * e
            tmat[k * size : (k + 1) * size, n * size : (n + 1) * size] = total.astype(bf16)

    loads[1].wait()
    blk = 64
    r = lax.broadcasted_iota(jnp.int32, (basis * blk, basis * blk), 0)
    col = lax.broadcasted_iota(jnp.int32, (basis * blk, basis * blk), 1)
    kk = (r >= blk).astype(jnp.int32) + (r >= 2 * blk).astype(jnp.int32)
    perm = jnp.where(col == 3 * (r - blk * kk) + kk, 1.0, 0.0).astype(bf16)
    for b in range(chans // blk):
        part = dot(perm, w[b * basis * blk : (b + 1) * basis * blk, :], 1, 0).astype(bf16)
        for k in range(basis):
            wk[k, b * blk : (b + 1) * blk, :] = part[k * blk : (k + 1) * blk, :]

    loads[2].wait()
    loads[3].wait()

    @pl.when(lat > 0)
    def _():
        down.wait_recv()

    @pl.when(lat < last)
    def _():
        up.wait_recv()

    bas[0] = dot(tmat[...], xs[...].reshape(3 * size, chans), 1, 0).astype(bf16)
    send_bas = remote(bas.at[0], bas.at[1], fac_s.at[0], fac_r.at[0], (c_lat, dp))
    send_bas.start()
    mixed = dot(bas[0, 0:size, :], wk[0], 1, 0)
    for k in range(1, basis):
        mixed = mixed + dot(bas[0, k * size : (k + 1) * size, :], wk[k], 1, 0)
    gate = jax.nn.sigmoid(mixed)
    dmix[0] = (cot[...].astype(f32) * gate * (1.0 + mixed * (1.0 - gate))).astype(bf16)
    send_dmix = remote(dmix.at[0], dmix.at[1], fac_s.at[1], fac_r.at[1], (c_lat, dp))
    send_dmix.start()
    out_ref[0, 0] = (xs[0].astype(f32) + mixed * gate).astype(bf16)

    dm = dmix[0]
    for k in range(basis):
        dbas[k * size : (k + 1) * size, :] = dot(dm, wk[k], 1, 1).astype(bf16)

    send_bas.wait_recv()
    send_dmix.wait_recv()
    both = dmix[...].reshape(2 * size, chans)

    def exchange(h):
        gt, r1 = gts[h], r1s[h]
        ends = (
            (2, gt.at[1 - y, x_lat], (x_lat, y_dp)),
            (0, gt.at[y, x_lat], (x_lat, dp)),
            (1, gt.at[1 - y, lat], (lat, y_dp)),
        )
        copies = [remote(src, r1.at[n], xy_s.at[3 * h + n], xy_r.at[3 * h + n], to) for n, src, to in ends]
        for copy in copies:
            copy.start()
        return copies

    xy = [None, None]
    for k in range(basis):
        lhs = jnp.concatenate([bas[0, k * size : (k + 1) * size, :], bas[1, k * size : (k + 1) * size, :]], axis=0)
        grad = dot(lhs, both, 0, 0).astype(bf16)
        for d in range(8):
            for i in range(3):
                for j in range(3):
                    at, part = divmod((k * 3 + i) * 3 + j, 4)
                    h, at = (0, at) if at < CHUNKS[0] else (1, at - CHUNKS[0])
                    lo = 48 * d + TILE * i
                    gts[h][d % 2, part, d // 2, at * TILE : (at + 1) * TILE, :] = grad[
                        lo : lo + TILE, j * LANES : (j + 1) * LANES
                    ]
        if k == 1:
            xy[0] = exchange(0)
    xy[1] = exchange(1)

    back[...] = dot(tmat[...], dbas[...], 0, 0)
    rim[0] = back[size : 2 * size, :].astype(bf16)
    rim[1] = back[2 * size : 3 * size, :].astype(bf16)
    rim_up = remote(rim.at[0], rim.at[3], rim_s.at[0], rim_r.at[0], (lat - 1, dp))
    rim_down = remote(rim.at[1], rim.at[2], rim_s.at[1], rim_r.at[1], (lat + 1, dp))

    zs = []
    for h in range(2):
        for copy in xy[h]:
            copy.wait_recv()
        own, r1, s1, r2 = gts[h].at[y, lat], r1s[h], s1s[h], r2s[h]
        sends = []
        for o in (2, 1, 3, 4):
            n = (z + o) % 4
            s1[n] = (
                own[n].astype(f32) + r1[0, n].astype(f32) + (r1[1, n].astype(f32) + r1[2, n].astype(f32))
            ).astype(bf16)
            if o < 4:
                copy = remote(
                    s1.at[n], r2.at[o - 1], z_s.at[3 * h + o - 1], z_r.at[3 * h + o - 1], (lat, z_dps[o - 1])
                )
                copy.start()
                sends.append(copy)
        zs.append(sends)

    @pl.when(lat > 0)
    def _():
        rim_up.start()

    @pl.when(lat < last)
    def _():
        rim_down.start()

    lats, arrive = [], []
    for h in range(2):
        for copy in zs[h]:
            copy.wait_recv()
        s1, r2, q = s1s[h], r2s[h], qs[h]
        q[lat] = (
            s1[z].astype(f32) + r2[0].astype(f32) + (r2[1].astype(f32) + r2[2].astype(f32))
        ).astype(bf16)
        for n, other in ((2, xc_lat), (0, x_lat), (1, c_lat)):
            copy = remote(q.at[lat], q.at[lat], lat_s.at[3 * h + n], lat_r.at[3 * h + n], (other, dp))
            copy.start()
            lats.append(copy)
            arrive.append(
                remote(q.at[other], q.at[other], lat_s.at[3 * h + n], lat_r.at[3 * h + n], (other, dp))
            )
    @pl.when(lat < last)
    def _():
        rim_up.wait_recv()

    @pl.when(lat > 0)
    def _():
        rim_down.wait_recv()

    gin_ref[0, 0] = (
        cot[...].astype(f32) + back[0:size, :] + rim[2].astype(f32) + rim[3].astype(f32)
    ).astype(bf16)

    rr = lax.broadcasted_iota(jnp.int32, (144, 144), 0)
    cc = lax.broadcasted_iota(jnp.int32, (144, 144), 1)
    kc = (cc >= 48).astype(jnp.int32) + (cc >= 96).astype(jnp.int32)
    order = jnp.where(rr == 3 * (cc - 48 * kc) + kc, 1.0, 0.0).astype(bf16)
    factor = jnp.exp2(-scale_ref[...].astype(f32)) * (1.0 / math.sqrt(4 * 8 * size))
    jr = lax.broadcasted_iota(jnp.int32, (3, chans), 0)
    jc = lax.broadcasted_iota(jnp.int32, (3, chans), 1)
    spread = jnp.where(jnp.logical_and(jc >= jr * LANES, jc < (jr + 1) * LANES), 1.0, 0.0).astype(f32)
    factor = dot(factor, spread, 0, 0)
    for copy in arrive:
        copy.wait_recv()
    for t in range(27):
        at, part = divmod(t, 4)
        q, at = (q_a, at) if at < CHUNKS[0] else (q_b, at - CHUNKS[0])
        g, j = divmod(t, 3)
        gk[g * TILE : (g + 1) * TILE, j * LANES : (j + 1) * LANES] = q[part, at * TILE : (at + 1) * TILE, :]
    wg_ref[...] = dot(order, gk[...], 1, 0) * factor

    @pl.when(lat < last)
    def _():
        down.wait_send()
        rim_down.wait_send()

    @pl.when(lat > 0)
    def _():
        up.wait_send()
        rim_up.wait_send()

    for copy in [send_bas, send_dmix] + xy[0] + xy[1] + zs[0] + zs[1] + lats:
        copy.wait_send()


def deliver(a_ref, b_ref, c_ref, a_out, b_out, c_out, sems):
    pairs = ((a_ref, a_out), (b_ref, b_out), (c_ref, c_out))
    copies = [pltpu.make_async_copy(src, dst, sems.at[n]) for n, (src, dst) in enumerate(pairs)]
    for copy in copies:
        copy.start()
    for copy in copies:
        copy.wait()


def local_fused(inputs, cotangent, kernel_tiles, mix_weight, slot_row, slot_lon, slot_count, scale_exps):
    size, chans = inputs.shape[2], inputs.shape[3]
    basis = kernel_tiles.shape[2]
    bf16, f32 = jnp.bfloat16, jnp.float32
    dma = pltpu.SemaphoreType.DMA
    vmem = pl.BlockSpec(memory_space=pltpu.VMEM)
    smem = pl.BlockSpec(memory_space=pltpu.SMEM)
    hbm = pl.BlockSpec(memory_space=pltpu.HBM)
    results = pl.pallas_call(
        fused,
        out_shape=(
            pltpu.VMEM(inputs.shape, bf16),
            pltpu.VMEM(inputs.shape, bf16),
            pltpu.VMEM((basis * chans // 8, chans), f32),
        ),
        in_specs=[smem, smem, vmem, hbm, hbm, hbm, hbm],
        out_specs=(vmem, vmem, vmem),
        scratch_shapes=[
            pltpu.VMEM((3, size, chans), bf16),
            pltpu.VMEM((size, chans), bf16),
            pltpu.VMEM(kernel_tiles.shape[1:], bf16),
            pltpu.VMEM(mix_weight.shape, bf16),
            pltpu.VMEM((basis, chans, chans), bf16),
            pltpu.VMEM((basis * size, 3 * size), bf16),
            pltpu.VMEM((2, basis * size, chans), bf16),
            pltpu.VMEM((2, size, chans), bf16),
            pltpu.VMEM((basis * size, chans), bf16),
            pltpu.VMEM((3 * size, chans), f32),
            pltpu.VMEM((4, size, chans), bf16),
            *[pltpu.VMEM((2, 4, 4, n * TILE, LANES), bf16) for n in CHUNKS],
            *[pltpu.VMEM((3, 4, n * TILE, LANES), bf16) for n in CHUNKS],
            *[pltpu.VMEM((4, n * TILE, LANES), bf16) for n in CHUNKS],
            *[pltpu.VMEM((3, n * TILE, LANES), bf16) for n in CHUNKS],
            *[pltpu.VMEM((4, n * TILE, LANES), bf16) for n in CHUNKS],
            pltpu.VMEM((144, chans), bf16),
            dma((4,)), dma((2,)), dma((2,)), dma((2,)), dma((2,)), dma((6,)), dma((6,)),
            dma((2,)), dma((2,)), dma((6,)), dma((6,)), dma((6,)), dma((6,)),
        ],
        compiler_params=pltpu.CompilerParams(
            collective_id=0, has_side_effects=True, vmem_limit_bytes=64960 * 1024
        ),
        cost_estimate=pl.CostEstimate(flops=10**9, bytes_accessed=3 * 10**6, transcendentals=50000),
    )(slot_row, slot_count, scale_exps.T, inputs, cotangent, kernel_tiles, mix_weight)
    return pl.pallas_call(
        deliver,
        out_shape=tuple(jax.ShapeDtypeStruct(one.shape, one.dtype) for one in results),
        in_specs=[pl.BlockSpec(memory_space=pl.ANY)] * 3,
        compiler_params=pltpu.CompilerParams(vmem_limit_bytes=32 * 1024 * 1024),
        out_specs=(hbm,) * 3,
        scratch_shapes=[dma((3,))],
    )(*results)


def fits(mesh):
    return mesh.shape["lat"] == 4 and mesh.shape["dp"] == 8


def solution(mesh):
    in_specs = (
        P("dp", "lat", None, None),
        P("dp", "lat", None, None),
        P("lat", None, None, None, None),
        P(),
        P("lat", None),
        P("lat", None),
        P("lat"),
        P("dp", None),
    )
    out_specs = (P("dp", "lat", None, None), P("dp", "lat", None, None), P("dp", None))
    body = local_fused if fits(mesh) else local
    return jax.shard_map(body, mesh=mesh, in_specs=in_specs, out_specs=out_specs, check_vma=False)
```

```python
import math

import jax
import jax.numpy as jnp
from jax import lax
from jax.experimental import pallas as pl
from jax.experimental.pallas import tpu as pltpu
from jax.sharding import PartitionSpec as P


def extended_2(cells, sides, width):
    for axis, dim in sides:
        count = lax.axis_size(axis)
        ends = count - 1
        head = lax.slice_in_dim(cells, 0, width, axis=dim)
        tail = lax.slice_in_dim(cells, cells.shape[dim] - width, cells.shape[dim], axis=dim)
        cells = jnp.concatenate(
            [
                lax.ppermute(tail, axis, [(i, (i + 1) % count) for i in range(ends)]),
                cells,
                lax.ppermute(head, axis, [((i + 1) % count, i) for i in range(ends)]),
            ],
            axis=dim,
        )
    return cells


def local(inputs, cotangent, kernel_tiles, mix_weight, slot_row, slot_lon, slot_count, scale_exps):
    rows_here = inputs.shape[1]
    lon_width = inputs.shape[2]
    channels = inputs.shape[3]
    slot_total = kernel_tiles.shape[1]
    basis_count = kernel_tiles.shape[2]
    tile_size = kernel_tiles.shape[3]
    lon_blocks = lon_width // tile_size
    points = rows_here * lon_width
    mix_major = (
        mix_weight.reshape(channels, basis_count, channels)
        .transpose(1, 0, 2)
        .reshape(basis_count * channels, channels)
    )
    extended = extended_2(inputs, (("lat", 1),), 1)
    blocks = extended[0].reshape(rows_here + 2, lon_blocks, tile_size, channels)
    row_ids = jnp.arange(rows_here, dtype=jnp.int32)
    blk_ids = jnp.arange(lon_blocks, dtype=jnp.int32)
    sources = []
    shifts = []
    masked = []
    for slot_index in range(slot_total):
        sources.append(row_ids + slot_row[:, slot_index] + 1)
        shifts.append((blk_ids[None, :] + slot_lon[:, slot_index][:, None]) % lon_blocks)
        keep_mask = (slot_index < slot_count).astype(jnp.bfloat16)
        masked.append(kernel_tiles[:, slot_index] * keep_mask[:, None, None, None])
    accum = jnp.zeros((rows_here, lon_blocks, tile_size, basis_count, channels), jnp.float32)
    for slot_index in range(slot_total):
        picked = blocks[sources[slot_index][:, None], shifts[slot_index]]
        accum = accum + jnp.einsum(
            "rkpq,rjqc->rjpkc", masked[slot_index], picked, preferred_element_type=jnp.float32
        )
    basis_out = accum.reshape(points, basis_count * channels).astype(jnp.bfloat16)
    mixed = jnp.dot(basis_out, mix_major, preferred_element_type=jnp.float32)
    gate_value = jax.nn.sigmoid(mixed)
    flat_in = inputs.reshape(points, channels).astype(jnp.float32)
    result = (flat_in + mixed * gate_value).astype(jnp.bfloat16).reshape(inputs.shape)
    flat_cot = cotangent.reshape(points, channels).astype(jnp.float32)
    dmixed = (flat_cot * gate_value * (1.0 + mixed * (1.0 - gate_value))).astype(jnp.bfloat16)
    dbasis = lax.dot_general(
        dmixed, mix_major, (((1,), (1,)), ((), ())), preferred_element_type=jnp.float32
    ).astype(jnp.bfloat16)
    dbasis = dbasis.reshape(rows_here, lon_blocks, tile_size, basis_count, channels)
    back_ext = jnp.zeros((rows_here + 2, lon_blocks, tile_size, channels), jnp.float32)
    for slot_index in range(slot_total):
        slot_term = jnp.einsum(
            "rkpq,rjpkc->rjqc", masked[slot_index], dbasis, preferred_element_type=jnp.float32
        )
        back_ext = back_ext.at[sources[slot_index][:, None], shifts[slot_index]].add(slot_term)
    rim_rows = jnp.concatenate([back_ext[:1], back_ext[rows_here + 1 :]], axis=0).reshape(
        2, lon_width, channels
    )
    returned = extended_2(rim_rows.astype(jnp.bfloat16), (("lat", 0),), 1).astype(rim_rows.dtype)
    inner_grad = back_ext[1 : rows_here + 1].reshape(rows_here, lon_width, channels)
    inner_grad = inner_grad.at[0].add(returned[0])
    inner_grad = inner_grad.at[rows_here - 1].add(returned[3])
    grad_in = (cotangent[0].astype(jnp.float32) + inner_grad).astype(jnp.bfloat16)[None]
    major_part = lax.dot_general(
        basis_out, dmixed, (((0,), (0,)), ((), ())), preferred_element_type=jnp.float32
    )
    partial_value = (
        major_part.reshape(basis_count, channels, channels)
        .transpose(1, 0, 2)
        .reshape(channels * basis_count, channels)
    )
    row_part = lax.psum_scatter(partial_value, "dp", scatter_dimension=0, tiled=True)
    grad_total = lax.psum(row_part, "lat")
    factor = jnp.repeat(jnp.exp2(-scale_exps.astype(jnp.float32)), tile_size, axis=1)
    count_all = lax.axis_size("dp") * inputs.shape[0] * lax.axis_size("lat") * rows_here * lon_width
    weight_grad = grad_total * factor / math.sqrt(count_all)
    return (result, grad_in, weight_grad)


MESH = pl.DeviceIdType.MESH
TILE = 16
LANES = 128
CHUNKS = (4, 3)


def dot(a, b, da, db):
    return lax.dot_general(a, b, (((da,), (db,)), ((), ())), preferred_element_type=jnp.float32)


def fused(
    row_ref, count_ref, scale_ref, x_hbm, cot_hbm, tiles_hbm, w_hbm,
    out_ref, gin_ref, wg_ref,
    xs, cot, tiles, w, wk, tmat, bas, dmix, dbas, back, rim, gt_a, gt_b, r1_a, r1_b, s1_a, s1_b, r2_a, r2_b, q_a, q_b, gk,
    load_sem, halo_s, halo_r, fac_s, fac_r, xy_s, xy_r, rim_s, rim_r, z_s, z_r, lat_s, lat_r,
):
    lat = lax.axis_index("lat")
    dp = lax.axis_index("dp")
    last = 3
    x, c = lat // 2, lat % 2
    z, y = dp // 2, dp % 2
    slots, basis = tiles.shape[0], tiles.shape[1]
    size = tiles.shape[2]
    chans = w.shape[1]
    f32, bf16 = jnp.float32, jnp.bfloat16

    loads = [
        pltpu.make_async_copy(tiles_hbm.at[0], tiles, load_sem.at[0]),
        pltpu.make_async_copy(w_hbm, w, load_sem.at[1]),
        pltpu.make_async_copy(x_hbm.at[0, 0], xs.at[0], load_sem.at[2]),
        pltpu.make_async_copy(cot_hbm.at[0, 0], cot, load_sem.at[3]),
    ]
    barrier = pltpu.get_barrier_semaphore()
    x_lat = (1 - x) * 2 + c
    c_lat = x * 2 + (1 - c)
    xc_lat = 3 - lat
    y_dp = z * 2 + (1 - y)
    z_dps = [((z + o) % 4) * 2 + y for o in (1, 2, 3)]
    friends = [(x_lat, dp), (c_lat, dp), (xc_lat, dp), (lat, y_dp), (x_lat, y_dp)]
    friends += [(lat, d) for d in z_dps]
    for friend in friends:
        pl.semaphore_signal(barrier, inc=1, device_id=friend, device_id_type=MESH)
    loads[2].start()
    loads[0].start()
    loads[1].start()
    loads[3].start()
    pl.semaphore_wait(barrier, len(friends))

    def remote(src, dst, send, recv, target):
        return pltpu.make_async_remote_copy(
            src_ref=src, dst_ref=dst, send_sem=send, recv_sem=recv,
            device_id=target, device_id_type=MESH,
        )

    down = remote(x_hbm.at[0, 0], xs.at[1], halo_s.at[0], halo_r.at[0], (lat + 1, dp))
    up = remote(x_hbm.at[0, 0], xs.at[2], halo_s.at[1], halo_r.at[1], (lat - 1, dp))

    @pl.when(lat < last)
    def _():
        down.start()

    @pl.when(lat > 0)
    def _():
        up.start()

    @pl.when(lat == 0)
    def _():
        xs[1] = jnp.zeros(xs.shape[1:], bf16)
        rim[2] = jnp.zeros(rim.shape[1:], bf16)

    @pl.when(lat == last)
    def _():
        xs[2] = jnp.zeros(xs.shape[1:], bf16)
        rim[3] = jnp.zeros(rim.shape[1:], bf16)

    gts, r1s, s1s, r2s, qs = (gt_a, gt_b), (r1_a, r1_b), (s1_a, s1_b), (r2_a, r2_b), (q_a, q_b)
    gt_b[:, 3, :, 32:48, :] = jnp.zeros((2, 4, TILE, LANES), bf16)

    loads[0].wait()
    count = count_ref[0]
    offs = (0, -1, 1)
    weight = [
        [jnp.where(jnp.logical_and(row_ref[0, s] == d, s < count), 1.0, 0.0).astype(f32) for s in range(3, slots)]
        for d in offs
    ]
    for k in range(basis):
        extra = [tiles[s, k].astype(f32) for s in range(3, slots)]
        for n in range(3):
            total = tiles[n, k].astype(f32)
            for t, e in zip(weight[n], extra):
                total = total + t * e
            tmat[k * size : (k + 1) * size, n * size : (n + 1) * size] = total.astype(bf16)

    loads[1].wait()
    blk = 64
    r = lax.broadcasted_iota(jnp.int32, (basis * blk, basis * blk), 0)
    col = lax.broadcasted_iota(jnp.int32, (basis * blk, basis * blk), 1)
    kk = (r >= blk).astype(jnp.int32) + (r >= 2 * blk).astype(jnp.int32)
    perm = jnp.where(col == 3 * (r - blk * kk) + kk, 1.0, 0.0).astype(bf16)
    for b in range(chans // blk):
        part = dot(perm, w[b * basis * blk : (b + 1) * basis * blk, :], 1, 0).astype(bf16)
        for k in range(basis):
            wk[k, b * blk : (b + 1) * blk, :] = part[k * blk : (k + 1) * blk, :]

    loads[2].wait()
    loads[3].wait()
    middle = dot(tmat[:, 0:size], xs[0], 1, 0)

    @pl.when(lat > 0)
    def _():
        down.wait_recv()

    @pl.when(lat < last)
    def _():
        up.wait_recv()

    bas[0] = (middle + dot(tmat[:, size : 3 * size], xs[1:3].reshape(2 * size, chans), 1, 0)).astype(bf16)
    send_bas = remote(bas.at[0], bas.at[1], fac_s.at[0], fac_r.at[0], (c_lat, dp))
    send_bas.start()
    mixed = dot(bas[0, 0:size, :], wk[0], 1, 0)
    for k in range(1, basis):
        mixed = mixed + dot(bas[0, k * size : (k + 1) * size, :], wk[k], 1, 0)
    gate = jax.nn.sigmoid(mixed)
    dmix[0] = (cot[...].astype(f32) * gate * (1.0 + mixed * (1.0 - gate))).astype(bf16)
    send_dmix = remote(dmix.at[0], dmix.at[1], fac_s.at[1], fac_r.at[1], (c_lat, dp))
    send_dmix.start()
    out_ref[0, 0] = (xs[0].astype(f32) + mixed * gate).astype(bf16)

    dm = dmix[0]
    for k in range(basis):
        dbas[k * size : (k + 1) * size, :] = dot(dm, wk[k], 1, 1).astype(bf16)

    send_bas.wait_recv()
    send_dmix.wait_recv()
    both = dmix[...].reshape(2 * size, chans)

    def exchange(h):
        gt, r1 = gts[h], r1s[h]
        ends = (
            (2, gt.at[1 - y, x_lat], (x_lat, y_dp)),
            (0, gt.at[y, x_lat], (x_lat, dp)),
            (1, gt.at[1 - y, lat], (lat, y_dp)),
        )
        copies = [remote(src, r1.at[n], xy_s.at[3 * h + n], xy_r.at[3 * h + n], to) for n, src, to in ends]
        for copy in copies:
            copy.start()
        return copies

    xy = [None, None]
    for k in range(basis):
        lhs = jnp.concatenate([bas[0, k * size : (k + 1) * size, :], bas[1, k * size : (k + 1) * size, :]], axis=0)
        grad = dot(lhs, both, 0, 0).astype(bf16)
        for d in range(8):
            for i in range(3):
                for j in range(3):
                    at, part = divmod((k * 3 + i) * 3 + j, 4)
                    h, at = (0, at) if at < CHUNKS[0] else (1, at - CHUNKS[0])
                    lo = 48 * d + TILE * i
                    gts[h][d % 2, part, d // 2, at * TILE : (at + 1) * TILE, :] = grad[
                        lo : lo + TILE, j * LANES : (j + 1) * LANES
                    ]
        if k == 1:
            xy[0] = exchange(0)
    xy[1] = exchange(1)

    back[...] = dot(tmat[...], dbas[...], 0, 0)
    rim[0] = back[size : 2 * size, :].astype(bf16)
    rim[1] = back[2 * size : 3 * size, :].astype(bf16)
    rim_up = remote(rim.at[0], rim.at[3], rim_s.at[0], rim_r.at[0], (lat - 1, dp))
    rim_down = remote(rim.at[1], rim.at[2], rim_s.at[1], rim_r.at[1], (lat + 1, dp))

    zs = []
    for h in range(2):
        for copy in xy[h]:
            copy.wait_recv()
        own, r1, s1, r2 = gts[h].at[y, lat], r1s[h], s1s[h], r2s[h]
        sends = []
        for o in (2, 1, 3, 4):
            n = (z + o) % 4
            s1[n] = (
                own[n].astype(f32) + r1[0, n].astype(f32) + (r1[1, n].astype(f32) + r1[2, n].astype(f32))
            ).astype(bf16)
            if o < 4:
                copy = remote(
                    s1.at[n], r2.at[o - 1], z_s.at[3 * h + o - 1], z_r.at[3 * h + o - 1], (lat, z_dps[o - 1])
                )
                copy.start()
                sends.append(copy)
        zs.append(sends)

    @pl.when(lat > 0)
    def _():
        rim_up.start()

    @pl.when(lat < last)
    def _():
        rim_down.start()

    lats, arrive = [], []
    for h in range(2):
        for copy in zs[h]:
            copy.wait_recv()
        s1, r2, q = s1s[h], r2s[h], qs[h]
        q[lat] = (
            s1[z].astype(f32) + r2[0].astype(f32) + (r2[1].astype(f32) + r2[2].astype(f32))
        ).astype(bf16)
        for n, other in ((2, xc_lat), (0, x_lat), (1, c_lat)):
            copy = remote(q.at[lat], q.at[lat], lat_s.at[3 * h + n], lat_r.at[3 * h + n], (other, dp))
            copy.start()
            lats.append(copy)
            arrive.append(
                remote(q.at[other], q.at[other], lat_s.at[3 * h + n], lat_r.at[3 * h + n], (other, dp))
            )
    @pl.when(lat < last)
    def _():
        rim_up.wait_recv()

    @pl.when(lat > 0)
    def _():
        rim_down.wait_recv()

    gin_ref[0, 0] = (
        cot[...].astype(f32) + back[0:size, :] + rim[2].astype(f32) + rim[3].astype(f32)
    ).astype(bf16)

    rr = lax.broadcasted_iota(jnp.int32, (144, 144), 0)
    cc = lax.broadcasted_iota(jnp.int32, (144, 144), 1)
    kc = (cc >= 48).astype(jnp.int32) + (cc >= 96).astype(jnp.int32)
    order = jnp.where(rr == 3 * (cc - 48 * kc) + kc, 1.0, 0.0).astype(bf16)
    factor = jnp.exp2(-scale_ref[...].astype(f32)) * (1.0 / math.sqrt(4 * 8 * size))
    jr = lax.broadcasted_iota(jnp.int32, (3, chans), 0)
    jc = lax.broadcasted_iota(jnp.int32, (3, chans), 1)
    spread = jnp.where(jnp.logical_and(jc >= jr * LANES, jc < (jr + 1) * LANES), 1.0, 0.0).astype(f32)
    factor = dot(factor, spread, 0, 0)
    for copy in arrive:
        copy.wait_recv()
    for t in range(27):
        at, part = divmod(t, 4)
        q, at = (q_a, at) if at < CHUNKS[0] else (q_b, at - CHUNKS[0])
        g, j = divmod(t, 3)
        gk[g * TILE : (g + 1) * TILE, j * LANES : (j + 1) * LANES] = q[part, at * TILE : (at + 1) * TILE, :]
    wg_ref[...] = dot(order, gk[...], 1, 0) * factor

    @pl.when(lat < last)
    def _():
        down.wait_send()
        rim_down.wait_send()

    @pl.when(lat > 0)
    def _():
        up.wait_send()
        rim_up.wait_send()

    for copy in [send_bas, send_dmix] + xy[0] + xy[1] + zs[0] + zs[1] + lats:
        copy.wait_send()


def deliver(a_ref, b_ref, c_ref, a_out, b_out, c_out, sems):
    pairs = ((a_ref, a_out), (b_ref, b_out), (c_ref, c_out))
    copies = [pltpu.make_async_copy(src, dst, sems.at[n]) for n, (src, dst) in enumerate(pairs)]
    for copy in copies:
        copy.start()
    for copy in copies:
        copy.wait()


def local_fused(inputs, cotangent, kernel_tiles, mix_weight, slot_row, slot_lon, slot_count, scale_exps):
    size, chans = inputs.shape[2], inputs.shape[3]
    basis = kernel_tiles.shape[2]
    bf16, f32 = jnp.bfloat16, jnp.float32
    dma = pltpu.SemaphoreType.DMA
    vmem = pl.BlockSpec(memory_space=pltpu.VMEM)
    smem = pl.BlockSpec(memory_space=pltpu.SMEM)
    hbm = pl.BlockSpec(memory_space=pltpu.HBM)
    results = pl.pallas_call(
        fused,
        out_shape=(
            pltpu.VMEM(inputs.shape, bf16),
            pltpu.VMEM(inputs.shape, bf16),
            pltpu.VMEM((basis * chans // 8, chans), f32),
        ),
        in_specs=[smem, smem, vmem, hbm, hbm, hbm, hbm],
        out_specs=(vmem, vmem, vmem),
        scratch_shapes=[
            pltpu.VMEM((3, size, chans), bf16),
            pltpu.VMEM((size, chans), bf16),
            pltpu.VMEM(kernel_tiles.shape[1:], bf16),
            pltpu.VMEM(mix_weight.shape, bf16),
            pltpu.VMEM((basis, chans, chans), bf16),
            pltpu.VMEM((basis * size, 3 * size), bf16),
            pltpu.VMEM((2, basis * size, chans), bf16),
            pltpu.VMEM((2, size, chans), bf16),
            pltpu.VMEM((basis * size, chans), bf16),
            pltpu.VMEM((3 * size, chans), f32),
            pltpu.VMEM((4, size, chans), bf16),
            *[pltpu.VMEM((2, 4, 4, n * TILE, LANES), bf16) for n in CHUNKS],
            *[pltpu.VMEM((3, 4, n * TILE, LANES), bf16) for n in CHUNKS],
            *[pltpu.VMEM((4, n * TILE, LANES), bf16) for n in CHUNKS],
            *[pltpu.VMEM((3, n * TILE, LANES), bf16) for n in CHUNKS],
            *[pltpu.VMEM((4, n * TILE, LANES), bf16) for n in CHUNKS],
            pltpu.VMEM((144, chans), bf16),
            dma((4,)), dma((2,)), dma((2,)), dma((2,)), dma((2,)), dma((6,)), dma((6,)),
            dma((2,)), dma((2,)), dma((6,)), dma((6,)), dma((6,)), dma((6,)),
        ],
        compiler_params=pltpu.CompilerParams(
            collective_id=0, has_side_effects=True, vmem_limit_bytes=64960 * 1024
        ),
        cost_estimate=pl.CostEstimate(flops=10**9, bytes_accessed=3 * 10**6, transcendentals=50000),
    )(slot_row, slot_count, scale_exps.T, inputs, cotangent, kernel_tiles, mix_weight)
    return pl.pallas_call(
        deliver,
        out_shape=tuple(jax.ShapeDtypeStruct(one.shape, one.dtype) for one in results),
        in_specs=[pl.BlockSpec(memory_space=pl.ANY)] * 3,
        compiler_params=pltpu.CompilerParams(vmem_limit_bytes=32 * 1024 * 1024),
        out_specs=(hbm,) * 3,
        scratch_shapes=[dma((3,))],
    )(*results)


def fits(mesh):
    return mesh.shape["lat"] == 4 and mesh.shape["dp"] == 8


def solution(mesh):
    in_specs = (
        P("dp", "lat", None, None),
        P("dp", "lat", None, None),
        P("lat", None, None, None, None),
        P(),
        P("lat", None),
        P("lat", None),
        P("lat"),
        P("dp", None),
    )
    out_specs = (P("dp", "lat", None, None), P("dp", "lat", None, None), P("dp", None))
    body = local_fused if fits(mesh) else local
    return jax.shard_map(body, mesh=mesh, in_specs=in_specs, out_specs=out_specs, check_vma=False)
```
